256 devices in a mesh: inner: 64 (over x, z, core), outer: 4 (over y).
Axes of the slice: x: 4, y: 4, z: 8, core: 2. Of those that a mesh axis runs over, the one named last changes fastest.
Arguments:
- queries: bfloat16 [4096, 768], P(('inner', 'outer')), may hold values from -8 to 8
- label_rows: float32 [131072, 768], P(('inner', 'outer')), may hold values from -3 to 3
- first_moment: float32 [131072, 768], P(('inner', 'outer')), may hold values from -0.015625 to 0.015625
- second_moment: float32 [131072, 768], P(('inner', 'outer')), may hold values from 1e-07 to 1e-05
- positive_ids: int32 [4096, 8], P(('inner', 'outer')), may hold values from 0 to 131071
- positive_counts: int32 [4096], P(('inner', 'outer')), may hold values from 1 to 8, as said below
Outputs:
- new_rows: float32 [131072, 768], P(('inner', 'outer'))
- new_first: float32 [131072, 768], P(('inner', 'outer'))
- new_second: float32 [131072, 768], P(('inner', 'outer'))
- query_grad: float32 [4096, 768], P(('inner', 'outer'))
- log_total: float32 [4096], P(('inner', 'outer'))
The draws below stay inside these ranges and needn't reach their ends.
Inputs may be any that keep to these rules, and one draw needn't show every extreme that they name: `positive_counts`: every query has 1 to 8 valid slots, and some query has 8.
All inputs are finite; a program needn't handle non-finite values.
Results may differ from the reference program's by a relative error of at most 0.0003.
The reference program's roundings to bfloat16 on the way (of `rows_bf` and `score_grad`) count: a program that leaves them out, or rounds other values in their place, can miss the bound.
Values may be sent and summed in bfloat16 or wider, within the bound.
A program may use at most 128 MiB of HBM per device.

```python
import math
import jax
import jax.numpy as jnp
from jax import lax

D = 768
LAB_DEV = 512
P_MAX = 8
LABELS = 131072
QUERIES = 4096


def plant_layout(key):
    query_key, label_key, sign_key, spread_key = jax.random.split(key, 4)
    picked_queries = jax.random.permutation(query_key, QUERIES)[:8].astype(jnp.int32)
    picked_labels = jax.random.permutation(label_key, LABELS)[:16].astype(jnp.int32)
    signs = (2 * jax.random.randint(sign_key, (8, D), 0, 2) - 1).astype(jnp.float32)
    spread = jax.random.uniform(spread_key, (8,), jnp.float32)
    return (picked_queries, picked_labels[:8], picked_labels[8:], signs, spread)


def plant_strength(spread, lowest, highest):
    strength = lowest + (highest - lowest) * spread
    return strength.at[0].set(highest)


def draw_queries(key, part):
    picked_queries, first_labels, second_labels, signs, spread = plant_layout(key)
    key = jax.random.fold_in(key, 11)
    base = jnp.clip(jax.random.normal(key, (QUERIES, D), jnp.float32), -6.0, 6.0)
    strength = plant_strength(spread, 3.0, 6.0)
    base = base.at[picked_queries].set(strength[:, None] * signs)
    return base.astype(jnp.bfloat16)


def draw_label_rows(key, part):
    picked_queries, first_labels, second_labels, signs, spread = plant_layout(key)
    key = jax.random.fold_in(key, 13)
    scale = D ** (-0.5)
    base = jnp.clip(jax.random.normal(key, (LABELS, D), jnp.float32), -6.0, 6.0) * scale
    widen = max(1, 768 // D)
    level = 0.0625 * widen
    column = jnp.arange(D) % 8
    pattern = jnp.where(column == 0, -1.0, jnp.where(column == 4, 3.0, 1.0)).astype(jnp.float32)
    pattern = pattern.at[jnp.array([1, 2, 3, 5, 6, 7])].set(1.0 - 1.0 / widen)
    base = base.at[first_labels].set(level * signs)
    base = base.at[second_labels].set(level * signs * pattern[None, :])
    return base.astype(jnp.float32)


def draw_positive_counts(key, part):
    key = jax.random.fold_in(key, 7)
    counts = jax.random.randint(key, (QUERIES,), 1, P_MAX + 1)
    return counts.at[0].set(P_MAX).astype(jnp.int32)


def with_ends(entries, own_key, smallest, largest):
    index_at = [jax.random.randint(jax.random.fold_in(own_key, axis), (), 0, length) for axis, length in enumerate(entries.shape)]
    longest = entries.shape.index(max(entries.shape))
    beside = index_at[:longest] + [(index_at[longest] + 1) % entries.shape[longest]] + index_at[longest + 1:]
    return entries.at[tuple(index_at)].set(smallest).at[tuple(beside)].set(largest)


def steps_of(key, extent, pieces, smallest, top_value):
    def one(position, shards_of):
        steps = jax.random.uniform(jax.random.fold_in(jax.random.fold_in(key, 6), position), (shards_of,), jnp.float32, smallest / len(pieces), top_value / len(pieces))
        return jnp.repeat(jnp.exp(steps), extent[position] // shards_of).reshape((-1,) + (1,) * (len(extent) - position - 1))

    level = one(*pieces[0])
    for cut in pieces[1:]:
        level = level * one(*cut)
    return level


def bell_draw(rng, shape, scale, most, cuts=(), held_as=jnp.bfloat16):
    factor_of = steps_of(rng, shape, cuts, -0.22, 0.18) if cuts else 1.0
    values = jax.random.normal(rng, shape, jnp.float32) * scale * factor_of
    return jnp.minimum(jnp.maximum(values, -most), most).astype(held_as)


def setup_inputs(seed: int = 0) -> dict:
    key_of = jax.random.split(jax.random.key(seed), 7)
    return {
        "queries": draw_queries(jax.random.fold_in(key_of[6], 71), 0),
        "label_rows": draw_label_rows(jax.random.fold_in(key_of[6], 71), 0),
        "first_moment": bell_draw(key_of[2], (LABELS, D), 0.001, 0.015625, ((0, 256),), jnp.float32),
        "second_moment": jnp.clip(jnp.exp(math.log(9.999999747378752e-06) - 4.6051701 * jax.random.uniform(key_of[3], (LABELS, D), jnp.float32) ** steps_of(key_of[3], (LABELS, D), ((0, 256),), -0.2, 0.2)), 1.0000000116860974e-07, 9.999999747378752e-06),
        "positive_ids": with_ends(jax.random.randint(key_of[4], (QUERIES, P_MAX), 0, LABELS), jax.random.fold_in(key_of[4], 1), 0, LABELS - 1).astype(jnp.int32),
        "positive_counts": draw_positive_counts(jax.random.fold_in(key_of[6], 71), 0),
    }


def targets_for(ids, counts, start, width):
    columns = start + jnp.arange(width, dtype=jnp.int32)[None, :]
    share = jnp.zeros((ids.shape[0], width), jnp.float32)
    for slot_index in range(ids.shape[1]):
        matched = (ids[:, slot_index:slot_index + 1] == columns) & (counts[:, None] > slot_index)
        share = share + matched.astype(jnp.float32)
    return share / counts[:, None].astype(jnp.float32)

def reference(queries, label_rows, first_moment, second_moment, positive_ids, positive_counts):
    width = LAB_DEV * 8
    blocks = LABELS // width
    rows_b = label_rows.reshape(blocks, width, D)
    first_b = first_moment.reshape(blocks, width, D)
    second_b = second_moment.reshape(blocks, width, D)

    def pass_one(carry, block):
        peak, total = carry
        scores = jnp.dot(queries, block.astype(jnp.bfloat16).T, preferred_element_type=jnp.float32)
        top = jnp.maximum(peak, lax.optimization_barrier(jnp.max(scores, axis=1)))
        total = total * jnp.exp(peak - top) + lax.optimization_barrier(jnp.sum(jnp.exp(scores - top[:, None]), axis=1))
        return ((top, total), None)
    start_peak = jnp.full((QUERIES,), -1e+30, jnp.float32)
    (peak, total), _ = lax.scan(pass_one, (start_peak, jnp.zeros((QUERIES,), jnp.float32)), rows_b)
    log_total = peak + jnp.log(total)

    def pass_two(summed, inputs):
        number, block, first, second = inputs
        rows_bf = block.astype(jnp.bfloat16)
        scores = jnp.dot(queries, rows_bf.T, preferred_element_type=jnp.float32)
        target = targets_for(positive_ids, positive_counts, (number * width).astype(jnp.int32), width)
        score_grad = (jnp.exp(scores - log_total[:, None]) - target).astype(jnp.bfloat16)
        row_grad = jnp.dot(score_grad.T, queries, preferred_element_type=jnp.float32)
        summed = summed + jnp.dot(score_grad, rows_bf, preferred_element_type=jnp.float32)
        new_first = 0.9 * first + 0.1 * row_grad
        new_second = 0.999 * second + 0.001 * row_grad * row_grad
        update = new_first / (1.0 - 0.9 ** 10) / (jnp.sqrt(new_second / (1.0 - 0.999 ** 10)) + 1e-08)
        return (summed, (block - 0.001 * update, new_first, new_second))
    numbers = jnp.arange(blocks, dtype=jnp.int32)
    query_grad, (new_rows, new_first, new_second) = lax.scan(pass_two, jnp.zeros((QUERIES, D), jnp.float32), (numbers, rows_b, first_b, second_b))
    return (new_rows.reshape(LABELS, D), new_first.reshape(LABELS, D), new_second.reshape(LABELS, D), query_grad, log_total)
```

```python
import functools

import jax
import jax.numpy as jnp
from jax import lax
from jax.experimental import pallas as pl
from jax.experimental.pallas import tpu as pltpu
from jax.sharding import PartitionSpec as P

X, Z = 4, 8
LANES = 128
MESH = pl.DeviceIdType.MESH
ORDERS = ("xyz", "yzx", "zxy")


class Place:
    def __init__(self, sizes):
        self.sizes = sizes
        inner = lax.axis_index("inner")
        self.core = lax.rem(inner, 2)
        self.at = {
            "x": inner // (2 * sizes["z"]),
            "z": lax.rem(inner // 2, sizes["z"]),
            "y": lax.axis_index("outer"),
        }

    def ring(self, axis, delta):
        n = self.sizes[axis]
        return lax.rem(self.at[axis] + delta % n, n)

    def device(self, axis, delta):
        at = dict(self.at)
        core = self.core
        if axis == "core":
            core = 1 - core
        else:
            at[axis] = self.ring(axis, delta)
        return ((at["x"] * self.sizes["z"] + at["z"]) * 2 + core, at["y"])


def slab(ref, half, fixed):
    whole = slice(None)
    first = whole if half is None else half
    return ref.at[(first, *(fixed.get(axis, whole) for axis in "xyz"))]


def steps_of(order, sizes):
    return [(phase, step) for phase, axis in enumerate(order) for step in range(1, sizes[axis] // 2 + 1)]


class Gather:
    def __init__(self, place, part, held, send, recv):
        self.place, self.held, self.send, self.recv = place, held.at[part], send.at[part], recv.at[part]
        self.order = ORDERS[part][::-1]
        self.sent = []

    def copy(self, phase, step, way, origin, device):
        axis = self.order[phase]
        reach = self.place.sizes[axis] // 2
        fixed = {later: self.place.at[later] for later in self.order[phase + 1 :]}
        fixed[axis] = origin
        block = slab(self.held, way if step == reach else None, fixed)
        return pltpu.make_async_remote_copy(
            src_ref=block, dst_ref=block,
            send_sem=self.send.at[phase, way, step - 1], recv_sem=self.recv.at[phase, way, step - 1],
            device_id=device, device_id_type=MESH,
        )

    def arrive(self, phase, step):
        axis = self.order[phase]
        for way, sign in enumerate((1, -1)):
            self.copy(phase, step, way, self.place.ring(axis, -sign * step), self.place.device(axis, sign)).wait_recv()

    def tick(self, phase, step):
        axis = self.order[phase]
        if step > 1:
            self.arrive(phase, step - 1)
        elif phase > 0:
            self.arrive(phase - 1, self.place.sizes[self.order[phase - 1]] // 2)
        for way, sign in enumerate((1, -1)):
            copy = self.copy(phase, step, way, self.place.ring(axis, -sign * (step - 1)), self.place.device(axis, sign))
            copy.start()
            self.sent.append(copy)

    def finish(self):
        last = len(self.order) - 1
        self.arrive(last, self.place.sizes[self.order[last]] // 2)


class Reduce:
    def __init__(self, place, part, total, landing, send, recv):
        self.place, self.total, self.landing = place, total.at[part], landing
        self.send, self.recv = send.at[part], recv.at[part]
        self.order = ORDERS[part]
        self.sent = []

    def block(self, phase, target, half):
        axis = self.order[phase]
        fixed = {done: self.place.at[done] for done in self.order[:phase]}
        fixed[axis] = target
        return slab(self.total, half, fixed)

    def copy(self, phase, step, way, sign):
        axis = self.order[phase]
        reach = self.place.sizes[axis] // 2
        half = way if step == 1 else None
        landed = self.landing[phase].at[way, step - 1]
        return pltpu.make_async_remote_copy(
            src_ref=self.block(phase, self.place.ring(axis, sign * (reach - step + 1)), half),
            dst_ref=landed.at[0] if step == 1 else landed,
            send_sem=self.send.at[phase, way, step - 1], recv_sem=self.recv.at[phase, way, step - 1],
            device_id=self.place.device(axis, sign), device_id_type=MESH,
        )

    def arrive(self, phase, step):
        axis = self.order[phase]
        reach = self.place.sizes[axis] // 2
        for way, sign in enumerate((1, -1)):
            self.copy(phase, step, way, sign).wait_recv()
            half = way if step == 1 else None
            mine = self.block(phase, self.place.ring(axis, sign * (reach - step)), half)
            landed = self.landing[phase].at[way, step - 1]
            if step == 1:
                landed = landed.at[0]
            mine[...] += landed[...]

    def tick(self, phase, step):
        if step > 1:
            self.arrive(phase, step - 1)
        elif phase > 0:
            self.arrive(phase - 1, self.place.sizes[self.order[phase - 1]] // 2)
        for way, sign in enumerate((1, -1)):
            copy = self.copy(phase, step, way, sign)
            copy.start()
            self.sent.append(copy)

    def finish(self):
        last = len(self.order) - 1
        self.arrive(last, self.place.sizes[self.order[last]] // 2)


def exchange(place, axis, source, slots, send, recv):
    copies = []
    for delta in range(1, place.sizes[axis]):
        copy = pltpu.make_async_remote_copy(
            src_ref=source, dst_ref=slots.at[delta - 1],
            send_sem=send.at[delta - 1], recv_sem=recv.at[delta - 1],
            device_id=place.device(axis, delta), device_id_type=MESH,
        )
        copy.start()
        copies.append(copy)
    return copies


def kernel(
    sizes, q_ref, rows_ref, ids_ref, row_grad_ref, query_grad_ref, log_ref,
    rows_bf, held, scores, grads, total, *rest,
):
    landings, rest = rest[:9], rest[9:]
    (ids_z, ids_y, ids_x, ids_zs, ids_ys, stat, stat_x, stat_y, stat_z, logs, factor, row_part, row_land,
     g_send, g_recv, r_send, r_recv, s_send, s_recv, i_send, i_recv, c_send, c_recv) = rest
    place = Place(sizes)
    nx, ny, nz = sizes["x"], sizes["y"], sizes["z"]
    width = rows_ref.shape[0]
    lanes = nz * 16
    at = place.at
    core = place.core

    barrier = pltpu.get_barrier_semaphore()
    peers = [("core", 1)] + [(axis, delta) for axis in "xyz" for delta in range(1, sizes[axis])]
    for axis, delta in peers:
        pl.semaphore_signal(barrier, inc=1, device_id=place.device(axis, delta), device_id_type=MESH)

    own = q_ref[...]
    for piece in range(6):
        held[piece // 2, piece % 2, at["x"], at["y"], at["z"]] = own[:, piece * LANES : (piece + 1) * LANES]
    lane = lax.broadcasted_iota(jnp.int32, (8, lanes), 1)
    own_ids = jnp.where(lane // 16 == at["z"], ids_ref[...], -1)
    ids_zs[...] = own_ids
    rows_bf[core] = rows_ref[...].astype(jnp.bfloat16)

    pl.semaphore_wait(barrier, len(peers))

    gathers = [Gather(place, part, held, g_send, g_recv) for part in range(3)]
    ticks = [steps_of(g.order, sizes) for g in gathers]
    sent = []
    id_copies = exchange(place, "z", ids_zs, ids_z, i_send.at[0], i_recv.at[0])
    sent += id_copies
    for k in range(len(ticks[0])):
        for g, steps in zip(gathers, ticks):
            g.tick(*steps[k])
        if k == 0:
            rows_copy = pltpu.make_async_remote_copy(
                src_ref=rows_bf.at[core], dst_ref=rows_bf.at[core], send_sem=c_send.at[0], recv_sem=c_recv.at[0],
                device_id=place.device("core", 1), device_id_type=MESH,
            )
            rows_copy.start()
        if k == 1:
            merged = own_ids
            for copy in id_copies:
                copy.wait_recv()
            for slot in range(nz - 1):
                merged = jnp.maximum(merged, ids_z[slot])
            ids_ys[at["y"]] = merged
            id_copies = []
            for delta in range(1, ny):
                copy = pltpu.make_async_remote_copy(
                    src_ref=ids_ys.at[at["y"]], dst_ref=ids_ys.at[at["y"]],
                    send_sem=i_send.at[1, delta - 1], recv_sem=i_recv.at[1, delta - 1],
                    device_id=place.device("y", delta), device_id_type=MESH,
                )
                copy.start()
                id_copies.append(copy)
            sent += id_copies
        if k == 2:
            for delta in range(1, ny):
                pltpu.make_async_remote_copy(
                    src_ref=ids_ys.at[at["y"]], dst_ref=ids_ys.at[place.ring("y", -delta)],
                    send_sem=i_send.at[1, delta - 1], recv_sem=i_recv.at[1, delta - 1],
                    device_id=place.device("y", delta), device_id_type=MESH,
                ).wait_recv()
            ids_x[at["x"]] = ids_ys[...]
            for delta in range(1, nx):
                copy = pltpu.make_async_remote_copy(
                    src_ref=ids_x.at[at["x"]], dst_ref=ids_x.at[at["x"]],
                    send_sem=i_send.at[2, delta - 1], recv_sem=i_recv.at[2, delta - 1],
                    device_id=place.device("x", delta), device_id_type=MESH,
                )
                copy.start()
                sent.append(copy)
    for g in gathers:
        g.finish()
    for delta in range(1, nx):
        pltpu.make_async_remote_copy(
            src_ref=ids_x.at[at["x"]], dst_ref=ids_x.at[place.ring("x", -delta)],
            send_sem=i_send.at[2, delta - 1], recv_sem=i_recv.at[2, delta - 1],
            device_id=place.device("x", delta), device_id_type=MESH,
        ).wait_recv()
    rows_copy.wait_recv()

    def queries_of(x, y, count):
        pieces = [held[p // 2, p % 2, x, pl.ds(y, count)].reshape(count * lanes, LANES) for p in range(6)]
        return jnp.concatenate(pieces, axis=1)

    def score_step(x, carry):
        for y in range(0, ny, 2):
            query = queries_of(x, y, 2)
            tops = []
            for side in range(2):
                block = lax.dot_general(
                    rows_bf[side], query, (((1,), (1,)), ((), ())), preferred_element_type=jnp.float32
                )
                tops.append(jnp.max(block, axis=0, keepdims=True))
                for k in range(2):
                    scores[x, y + k, side] = block[:, k * lanes : (k + 1) * lanes]
            top = jnp.maximum(tops[0], tops[1])
            for k in range(2):
                part = top[:, k * lanes : (k + 1) * lanes]
                amount = jnp.zeros((1, lanes), jnp.float32)
                for side in range(2):
                    power = jnp.exp(scores[x, y + k, side] - part)
                    scores[x, y + k, side] = power
                    amount += jnp.sum(power, axis=0, keepdims=True)
                stat[0, 0, x, pl.ds(y + k, 1)] = part
                stat[0, 1, x, pl.ds(y + k, 1)] = amount
        return carry

    lax.fori_loop(0, nx, score_step, 0)

    for stage, (axis, slots) in enumerate((("x", stat_x), ("y", stat_y), ("z", stat_z))):
        copies = exchange(place, axis, stat.at[stage], slots, s_send.at[stage], s_recv.at[stage])
        sent += copies
        for copy in copies:
            copy.wait_recv()
        count = sizes[axis] - 1
        top = stat[stage, 0]
        for slot in range(count):
            top = jnp.maximum(top, slots[slot, 0])
        amount = stat[stage, 1] * jnp.exp(stat[stage, 0] - top)
        for slot in range(count):
            amount += slots[slot, 1] * jnp.exp(slots[slot, 0] - top)
        if stage < 2:
            stat[stage + 1, 0] = top
            stat[stage + 1, 1] = amount
    log_total = top + jnp.log(amount)
    logs[...] = log_total
    factor[...] = jnp.exp(stat[0, 0] - log_total)
    log_ref[...] = jnp.broadcast_to(logs[at["x"], pl.ds(at["y"], 1)], (8, lanes))

    def grad_step(x, carry):
        for y in range(ny):
            ids = ids_x[x, y]
            share = 1.0 / jnp.sum((ids >= 0).astype(jnp.float32), axis=0, keepdims=True)
            scale = factor[x, pl.ds(y, 1)]
            for side in range(2):
                start = (((at["x"] * nz + at["z"]) * 2 + side) * ny + at["y"]) * width
                label = start + lax.broadcasted_iota(jnp.int32, (width, lanes), 0)
                hits = jnp.zeros((width, lanes), jnp.float32)
                for slot in range(8):
                    hits += jnp.where(ids[slot : slot + 1] == label, share, 0.0)
                grads[x, y, side] = (scores[x, y, side] * scale - hits).astype(jnp.bfloat16)
        return carry

    lax.fori_loop(0, nx, grad_step, 0)

    def query_step(x, carry):
        for y in range(0, ny, 2):
            out = None
            for side in range(2):
                left = jnp.concatenate([grads[x, y, side], grads[x, y + 1, side]], axis=1)
                term = lax.dot_general(
                    left, rows_bf[side], (((0,), (0,)), ((), ())), preferred_element_type=jnp.float32
                )
                out = term if out is None else out + term
            for piece in range(6):
                total[piece // 2, piece % 2, x, pl.ds(y, 2)] = out[
                    :, piece * LANES : (piece + 1) * LANES
                ].reshape(2, nz, 16, LANES)
        return carry

    lax.fori_loop(0, nx, query_step, 0)

    def row_side(side, out):
        out[...] = jnp.zeros(out.shape, jnp.float32)

        def step(x, carry):
            left = jnp.concatenate([grads[x, y, side] for y in range(ny)], axis=1)
            out[...] += jnp.dot(left, queries_of(x, 0, ny), preferred_element_type=jnp.float32)
            return carry

        lax.fori_loop(0, nx, step, 0)

    reduces = [
        Reduce(place, part, total, landings[3 * part : 3 * part + 3], r_send, r_recv) for part in range(3)
    ]
    ticks = [steps_of(r.order, sizes) for r in reduces]
    for k in range(len(ticks[0])):
        for r, steps in zip(reduces, ticks):
            r.tick(*steps[k])
        if k == 0:
            row_side(1 - core, row_part)
            row_copy = pltpu.make_async_remote_copy(
                src_ref=row_part, dst_ref=row_land, send_sem=c_send.at[1], recv_sem=c_recv.at[1],
                device_id=place.device("core", 1), device_id_type=MESH,
            )
            row_copy.start()
        if k == 1:
            row_side(core, row_grad_ref)
            row_copy.wait_recv()
            row_grad_ref[...] += row_land[...]
    for r in reduces:
        r.finish()
    for piece in range(6):
        query_grad_ref[:, piece * LANES : (piece + 1) * LANES] = total[
            piece // 2, piece % 2, at["x"], at["y"], at["z"]
        ]
    for group in (*gathers, *reduces):
        sent += group.sent
    for copy in (*sent, rows_copy, row_copy):
        copy.wait_send()


def exchange_step(queries, label_rows, lane_ids, sizes):
    nx, ny, nz = (sizes[axis] for axis in "xyz")
    width, depth = label_rows.shape
    lanes = nz * 16
    f32, bf16 = jnp.float32, jnp.bfloat16
    landings = []
    for order in ORDERS:
        for phase, axis in enumerate(order):
            rest = [sizes[a] for a in "xyz" if a in order[phase + 1 :]]
            landings.append(pltpu.VMEM((2, sizes[axis] // 2, 2, *rest, 16, LANES), f32))
    most = max(sizes.values())
    dma = pltpu.SemaphoreType.DMA
    vmem = pl.BlockSpec(memory_space=pltpu.VMEM)
    return pl.pallas_call(
        functools.partial(kernel, sizes),
        out_shape=(
            jax.ShapeDtypeStruct((width, depth), f32),
            jax.ShapeDtypeStruct((16, depth), f32),
            jax.ShapeDtypeStruct((8, lanes), f32),
        ),
        in_specs=[vmem] * 3,
        out_specs=(vmem,) * 3,
        scratch_shapes=[
            pltpu.VMEM((2, width, depth), bf16),
            pltpu.VMEM((3, 2, nx, ny, nz, 16, LANES), bf16),
            pltpu.VMEM((nx, ny, 2, width, lanes), f32),
            pltpu.VMEM((nx, ny, 2, width, lanes), bf16),
            pltpu.VMEM((3, 2, nx, ny, nz, 16, LANES), f32),
            *landings,
            pltpu.VMEM((nz - 1, 8, lanes), jnp.int32),
            pltpu.VMEM((1, 8, lanes), jnp.int32),
            pltpu.VMEM((nx, ny, 8, lanes), jnp.int32),
            pltpu.VMEM((8, lanes), jnp.int32),
            pltpu.VMEM((ny, 8, lanes), jnp.int32),
            pltpu.VMEM((3, 2, nx, ny, lanes), f32),
            pltpu.VMEM((nx - 1, 2, nx, ny, lanes), f32),
            pltpu.VMEM((ny - 1, 2, nx, ny, lanes), f32),
            pltpu.VMEM((nz - 1, 2, nx, ny, lanes), f32),
            pltpu.VMEM((nx, ny, lanes), f32),
            pltpu.VMEM((nx, ny, lanes), f32),
            pltpu.VMEM((width, depth), f32),
            pltpu.VMEM((width, depth), f32),
            dma((3, 3, 2, most // 2)), dma((3, 3, 2, most // 2)),
            dma((3, 3, 2, most // 2)), dma((3, 3, 2, most // 2)),
            dma((3, most)), dma((3, most)),
            dma((3, most)), dma((3, most)),
            dma((2,)), dma((2,)),
        ],
        compiler_params=pltpu.CompilerParams(
            collective_id=0, has_side_effects=True, vmem_limit_bytes=56 << 20
        ),
        name="classifier_step",
    )(queries, label_rows, lane_ids)


def adam_update(label_rows, first_moment, second_moment, row_grad):
    new_first = 0.9 * first_moment + 0.1 * row_grad
    new_second = 0.999 * second_moment + 0.001 * row_grad * row_grad
    update = new_first / (1.0 - 0.9**10) / (jnp.sqrt(new_second / (1.0 - 0.999**10)) + 1e-08)
    return (label_rows - 0.001 * update, new_first, new_second)


def shards(sizes, queries, label_rows, first_moment, second_moment, positive_ids, positive_counts):
    slots = jnp.arange(positive_ids.shape[1], dtype=jnp.int32)
    valid = jnp.where(slots[None, :] < positive_counts[:, None], positive_ids, -1)
    lane_ids = jnp.tile(valid.T, (1, sizes["z"]))
    row_grad, query_grad, logs = exchange_step(queries, label_rows, lane_ids, sizes)
    z = lax.rem(lax.axis_index("inner") // 2, sizes["z"])
    own_total = lax.dynamic_slice_in_dim(logs[0], z * 16, 16, 0)
    new_rows, new_first, new_second = adam_update(label_rows, first_moment, second_moment, row_grad)
    return (new_rows, new_first, new_second, query_grad, own_total)


def solution(mesh):
    sizes = {"x": X, "y": mesh.shape["outer"], "z": Z}
    rows = P(("inner", "outer"), None)
    return jax.shard_map(
        functools.partial(shards, sizes),
        mesh=mesh,
        in_specs=(rows, rows, rows, rows, rows, P(("inner", "outer"))),
        out_specs=(rows, rows, rows, rows, P(("inner", "outer"))),
        check_vma=False,
    )
```

```python
import functools
import heapq
import itertools

import jax
import jax.numpy as jnp
from jax import lax
from jax.experimental import pallas as pl
from jax.experimental.pallas import tpu as pltpu
from jax.sharding import PartitionSpec as P

X, Z = 4, 8
LANES = 128
MESH = pl.DeviceIdType.MESH
ORDERS = ("xyz", "yzx", "zxy")
LINK_RATE = 46.0
COPIES = 256


class Place:
    def __init__(self, sizes):
        self.sizes = sizes
        inner = lax.axis_index("inner")
        self.core = lax.rem(inner, 2)
        self.at = {
            "x": inner // (2 * sizes["z"]),
            "z": lax.rem(inner // 2, sizes["z"]),
            "y": lax.axis_index("outer"),
        }

    def ring(self, axis, delta):
        n = self.sizes[axis]
        return lax.rem(self.at[axis] + delta % n, n)

    def device(self, axis, delta):
        at = dict(self.at)
        core = self.core
        if axis == "core":
            core = 1 - core
        else:
            at[axis] = self.ring(axis, delta)
        return ((at["x"] * self.sizes["z"] + at["z"]) * 2 + core, at["y"])


def slab(ref, half, fixed):
    whole = slice(None)
    first = whole if half is None else half
    return ref.at[(first, *(fixed.get(axis, whole) for axis in "xyz"))]


def offsets(n):
    half = n // 2
    return [0, *(sign * d for d in range(1, half) for sign in (1, -1)), half]


class Message:
    def __init__(self, key, link, kib, hops, deps, copy, landed=None, arrive=None):
        self.key, self.link, self.kib, self.hops, self.deps = key, link, kib, hops, set(deps)
        self.copy, self.landed, self.arrive = copy, landed or copy, arrive


class Job:
    def __init__(self, key, cost, deps, work):
        self.key, self.cost, self.deps, self.work = key, cost, set(deps), work


def play(messages, jobs, leading=()):
    now, free, arrivals, done, sent = 0.0, {}, [], set(), []
    waiting, jobs, leading = list(messages), list(jobs), list(leading)

    def start_ready():
        for message in list(waiting):
            if message.deps <= done:
                waiting.remove(message)
                copy = message.copy()
                copy.start()
                sent.append(copy)
                begin = max(now, free.get(message.link, 0.0))
                free[message.link] = begin + message.kib * message.hops / LINK_RATE
                heapq.heappush(arrivals, (free[message.link] + 0.5 + 0.7 * message.hops, len(sent), message))

    def run(job):
        nonlocal now
        job.work()
        now += job.cost
        done.add(job.key)

    start_ready()
    for job in leading:
        run(job)
        start_ready()
    while arrivals or jobs:
        ready = [job for job in jobs if job.deps <= done]
        prompt = [job for job in ready if job.cost == 0]
        gap = arrivals[0][0] - now if arrivals else 1e9
        if prompt or (ready and gap > 0.6 * ready[0].cost):
            job = (prompt or ready)[0]
            jobs.remove(job)
            run(job)
        else:
            when, _, message = heapq.heappop(arrivals)
            now = max(now, when) + 0.05
            message.landed().wait_recv()
            if message.arrive is not None:
                message.arrive()
                now += message.kib / 2000
            done.add(message.key)
        start_ready()
    assert not waiting
    return sent


class Copies:
    def __init__(self, place, send, recv):
        self.place, self.send, self.recv, self.used = place, send, recv, 0

    def slot(self):
        self.used += 1
        return self.used - 1

    def copy(self, slot, source, target, axis, delta):
        return pltpu.make_async_remote_copy(
            src_ref=source, dst_ref=target, send_sem=self.send.at[slot], recv_sem=self.recv.at[slot],
            device_id=self.place.device(axis, delta), device_id_type=MESH,
        )


def gather_messages(copies, part, held):
    place = copies.place
    held = held.at[part]
    first, second, third = ORDERS[part][::-1]
    at, sizes = place.at, place.sizes
    out = []

    def add(key, axis, delta, kib, hops, deps, block_from):
        slot = copies.slot()
        make = lambda back: copies.copy(slot, block_from(back), block_from(back), axis, delta)
        out.append(Message(
            key, (axis, delta > 0), kib, hops, deps,
            functools.partial(make, 0), functools.partial(make, 1),
        ))

    base = 16 * 2 * LANES * 2 / 1024
    for delta in range(1, sizes[first]):
        far = min(delta, sizes[first] - delta)

        def block(back, delta=delta):
            fixed = dict(at)
            fixed[first] = place.ring(first, -delta * back)
            return slab(held, None, fixed)

        add((part, 1, delta), first, delta, base, far, (), block)
    start = [(part, 1, delta) for delta in range(1, sizes[first])]
    base *= sizes[first]
    reach = sizes[second] // 2
    for step in range(1, reach + 1):
        for way, sign in enumerate((1, -1)):

            def block(back, step=step, way=way, sign=sign):
                fixed = {third: at[third], second: place.ring(second, -sign * (step - 1 + back))}
                return slab(held, way if step == reach else None, fixed)

            deps = start if step == 1 else [(part, 2, way, step - 1)]
            add((part, 2, way, step), second, sign, base / (1 + (step == reach)), 1, deps, block)
    far = sizes[third] // 2
    for offset in offsets(sizes[second]):
        for step in range(1, far + 1):
            for way, sign in enumerate((1, -1)):

                def block(back, offset=offset, step=step, way=way, sign=sign):
                    fixed = {
                        second: place.ring(second, offset),
                        third: place.ring(third, -sign * (step - 1 + back)),
                    }
                    return slab(held, way if step == far else None, fixed)

                if step > 1:
                    deps = [(part, 3, offset, way, step - 1)]
                elif offset == 0:
                    deps = start
                elif abs(offset) == reach:
                    deps = [(part, 2, 0, reach), (part, 2, 1, reach)]
                else:
                    deps = [(part, 2, 0 if offset < 0 else 1, abs(offset))]
                add((part, 3, offset, way, step), third, sign, base / (1 + (step == far)), 1, deps, block)
    return out


def reduce_messages(copies, part, total, landings):
    place = copies.place
    total = total.at[part]
    first, second, third = ORDERS[part]
    at, sizes = place.at, place.sizes
    out = []

    def add(key, axis, delta, kib, hops, deps, source, landed, mine):
        slot = copies.slot()

        def arrive():
            mine()[...] += landed[...]

        out.append(Message(
            key, (axis, delta > 0), kib, hops, deps,
            lambda: copies.copy(slot, source(), landed, axis, delta), None, arrive,
        ))

    base = sizes[third] * 16 * 2 * LANES * 4 / 1024
    reach, far = sizes[first] // 2, sizes[second] // 2
    for number, offset in enumerate(offsets(sizes[second])[::-1]):
        for step in range(1, reach + 1):
            for way, sign in enumerate((1, -1)):

                def block(ahead, offset=offset, step=step, way=way, sign=sign):
                    fixed = {
                        second: place.ring(second, offset),
                        first: place.ring(first, sign * (reach - step + ahead)),
                    }
                    return slab(total, way if step == 1 else None, fixed)

                landed = landings[0].at[number, way, step - 1]
                if step == 1:
                    landed = landed.at[0]
                deps = [(part, 1, offset, way, step - 1)] if step > 1 else []
                ahead = sign * (reach - step + 1)
                planes = [reach if ahead == -reach else ahead] if first == "x" else offsets(sizes["x"])
                deps += [("query", plane) for plane in planes]
                add((part, 1, offset, way, step), first, sign, base / (1 + (step == 1)), 1, deps,
                    functools.partial(block, 1), landed, functools.partial(block, 0))
    for step in range(1, far + 1):
        for way, sign in enumerate((1, -1)):

            def block(ahead, step=step, way=way, sign=sign):
                fixed = {first: at[first], second: place.ring(second, sign * (far - step + ahead))}
                return slab(total, way if step == 1 else None, fixed)

            landed = landings[1].at[way, step - 1]
            if step == 1:
                landed = landed.at[0]
            offset = sign * (far - step + 1)
            if offset == -far:
                offset = far
            deps = [(part, 1, offset, w, reach) for w in range(2)]
            if step > 1:
                deps.append((part, 2, way, step - 1))
            add((part, 2, way, step), second, sign, base / (1 + (step == 1)), 1, deps,
                functools.partial(block, 1), landed, functools.partial(block, 0))
    base /= sizes[third]
    deps = [(part, 1, 0, w, reach) for w in range(2)] + [(part, 2, w, far) for w in range(2)]
    for delta in range(1, sizes[third]):

        def block(ahead, delta=delta):
            fixed = dict(at)
            fixed[third] = place.ring(third, delta * ahead)
            return slab(total, None, fixed)

        add((part, 3, delta), third, delta, base, min(delta, sizes[third] - delta), deps,
            functools.partial(block, 1), landings[2].at[delta - 1], functools.partial(block, 0))
    return out


def exchange(place, axis, source, slots, send, recv):
    copies = []
    for delta in range(1, place.sizes[axis]):
        copy = pltpu.make_async_remote_copy(
            src_ref=source, dst_ref=slots.at[delta - 1],
            send_sem=send.at[delta - 1], recv_sem=recv.at[delta - 1],
            device_id=place.device(axis, delta), device_id_type=MESH,
        )
        copy.start()
        copies.append(copy)
    return copies


def kernel(
    sizes, q_ref, rows_ref, ids_ref, row_grad_ref, query_grad_ref, log_ref,
    rows_bf, held, scores, grads, total, *rest,
):
    landings, rest = rest[:9], rest[9:]
    (ids_z, ids_x, ids_own, ids_ys, stat, stat_x, stat_y, stat_z, logs, factor, row_part, row_land,
     send, recv, s_send, s_recv) = rest
    place = Place(sizes)
    nx, ny, nz = sizes["x"], sizes["y"], sizes["z"]
    width = rows_ref.shape[0]
    lanes = nz * 16
    at = place.at
    core = place.core

    barrier = pltpu.get_barrier_semaphore()
    peers = [("core", 1)] + [(axis, delta) for axis in "xyz" for delta in range(1, sizes[axis])]
    for axis, delta in peers:
        pl.semaphore_signal(barrier, inc=1, device_id=place.device(axis, delta), device_id_type=MESH)

    own = q_ref[...]
    for piece in range(6):
        held[piece // 2, piece % 2, at["x"], at["y"], at["z"]] = own[:, piece * LANES : (piece + 1) * LANES]
    lane = lax.broadcasted_iota(jnp.int32, (8, lanes), 1)
    ids_own[...] = jnp.where(lane // 16 == at["z"], ids_ref[...], -1)
    rows_bf[core] = rows_ref[...].astype(jnp.bfloat16)

    pl.semaphore_wait(barrier, len(peers))

    copies = Copies(place, send, recv)

    def merge_ids():
        merged = ids_own[...]
        for slot in range(nz - 1):
            merged = jnp.maximum(merged, ids_z[slot])
        ids_ys[at["y"]] = merged

    def spread_ids():
        ids_x[at["x"]] = ids_ys[...]

    def count_hits(x):
        def step(y, carry):
            ids = ids_x[x, y]
            for side in range(2):
                start = (((at["x"] * nz + at["z"]) * 2 + side) * ny + at["y"]) * width
                label = start + lax.broadcasted_iota(jnp.int32, (width, lanes), 0)
                hits = jnp.zeros((width, lanes), jnp.float32)
                for slot in range(8):
                    hits += jnp.where(ids[slot : slot + 1] == label, 1.0, 0.0)
                grads[x, y, side] = hits.astype(jnp.bfloat16)
            return carry

        lax.fori_loop(0, ny, step, 0)

    def id_message(kind, axis, delta, kib, source, target, deps):
        slot = copies.slot()
        return Message(
            (kind, delta), (axis, True), kib, min(delta, sizes[axis] - delta), deps,
            lambda: copies.copy(slot, source, target(0), axis, delta),
            lambda: copies.copy(slot, source, target(1), axis, delta),
        )

    messages = [
        id_message("ids1", "z", delta, 4, ids_own, lambda back, delta=delta: ids_z.at[delta - 1], ())
        for delta in range(1, nz)
    ]
    messages += [
        id_message("ids2", "y", delta, 4, ids_ys.at[at["y"]],
                   lambda back, delta=delta: ids_ys.at[place.ring("y", -delta * back)], ["merge"])
        for delta in range(1, ny)
    ]
    messages += [
        id_message("ids3", "x", delta, 16, ids_x.at[at["x"]],
                   lambda back, delta=delta: ids_x.at[place.ring("x", -delta * back)], ["spread"])
        for delta in range(1, nx)
    ]
    parts = [gather_messages(copies, part, held) for part in range(3)]
    messages += [m for group in itertools.zip_longest(*parts) for m in group if m is not None]
    rows_slot = copies.slot()

    def rows_copy():
        return copies.copy(rows_slot, rows_bf.at[core], rows_bf.at[core], "core", 1)

    def rows_landed():
        return copies.copy(rows_slot, rows_bf.at[1 - core], rows_bf.at[1 - core], "core", 1)

    messages.append(Message("rows", ("core", True), width * 1.5 / 4, 1, (), rows_copy, rows_landed))
    jobs = [
        Job("merge", 0, [("ids1", delta) for delta in range(1, nz)], merge_ids),
        Job("spread", 0, ["merge", *(("ids2", delta) for delta in range(1, ny))], spread_ids),
        *(
            Job(("hits", x), 1.5, ["spread", *(("ids3", delta) for delta in range(1, nx))],
                functools.partial(count_hits, x))
            for x in range(nx)
        ),
    ]
    sent = play(messages, jobs)

    def queries_of(x, y, count):
        pieces = [held[p // 2, p % 2, x, pl.ds(y, count)].reshape(count * lanes, LANES) for p in range(6)]
        return jnp.concatenate(pieces, axis=1)

    def score_step(x, carry):
        for y in range(0, ny, 2):
            query = queries_of(x, y, 2)
            tops = []
            for side in range(2):
                block = lax.dot_general(
                    rows_bf[side], query, (((1,), (1,)), ((), ())), preferred_element_type=jnp.float32
                )
                tops.append(jnp.max(block, axis=0, keepdims=True))
                for k in range(2):
                    scores[x, y + k, side] = block[:, k * lanes : (k + 1) * lanes]
            top = jnp.maximum(tops[0], tops[1])
            for k in range(2):
                part = top[:, k * lanes : (k + 1) * lanes]
                amount = jnp.zeros((1, lanes), jnp.float32)
                for side in range(2):
                    power = jnp.exp(scores[x, y + k, side] - part)
                    scores[x, y + k, side] = power
                    amount += jnp.sum(power, axis=0, keepdims=True)
                stat[0, 0, x, pl.ds(y + k, 1)] = part
                stat[0, 1, x, pl.ds(y + k, 1)] = amount
        return carry

    lax.fori_loop(0, nx, score_step, 0)

    for stage, (axis, slots) in enumerate((("x", stat_x), ("y", stat_y), ("z", stat_z))):
        started = exchange(place, axis, stat.at[stage], slots, s_send.at[stage], s_recv.at[stage])
        sent += started
        for copy in started:
            copy.wait_recv()
        count = sizes[axis] - 1
        top = stat[stage, 0]
        for slot in range(count):
            top = jnp.maximum(top, slots[slot, 0])
        amount = stat[stage, 1] * jnp.exp(stat[stage, 0] - top)
        for slot in range(count):
            amount += slots[slot, 1] * jnp.exp(slots[slot, 0] - top)
        if stage < 2:
            stat[stage + 1, 0] = top
            stat[stage + 1, 1] = amount
    log_total = top + jnp.log(amount)
    logs[...] = log_total
    factor[...] = jnp.exp(stat[0, 0] - log_total)
    log_ref[...] = jnp.broadcast_to(logs[at["x"], pl.ds(at["y"], 1)], (8, lanes))

    def query_plane(offset):
        x = place.ring("x", offset)

        def step(pair, carry):
            y = 2 * pair
            out = None
            for side in range(2):
                for k in range(2):
                    share = 1.0 / jnp.sum((ids_x[x, y + k] >= 0).astype(jnp.float32), axis=0, keepdims=True)
                    scale = factor[x, pl.ds(y + k, 1)]
                    hits = grads[x, y + k, side].astype(jnp.float32)
                    grads[x, y + k, side] = (scores[x, y + k, side] * scale - hits * share).astype(jnp.bfloat16)
                left = jnp.concatenate([grads[x, y, side], grads[x, y + 1, side]], axis=1)
                term = lax.dot_general(
                    left, rows_bf[side], (((0,), (0,)), ((), ())), preferred_element_type=jnp.float32
                )
                out = term if out is None else out + term
            for piece in range(6):
                total[piece // 2, piece % 2, x, pl.ds(y, 2)] = out[
                    :, piece * LANES : (piece + 1) * LANES
                ].reshape(2, nz, 16, LANES)
            return carry

        lax.fori_loop(0, ny // 2, step, 0)

    def row_step(side, out, x):
        left = jnp.concatenate([grads[x, y, side] for y in range(ny)], axis=1)
        term = jnp.dot(left, queries_of(x, 0, ny), preferred_element_type=jnp.float32)
        if x == 0:
            out[...] = term
        else:
            out[...] += term

    def row_sum():
        row_grad_ref[...] += row_land[...]

    parts = [
        reduce_messages(copies, part, total, landings[3 * part : 3 * part + 3]) for part in range(3)
    ]
    messages = [m for group in itertools.zip_longest(*parts) for m in group if m is not None]
    row_slot = copies.slot()
    messages.append(Message(
        "row", ("core", True), width * 3 / 4, 1, [("theirs", x) for x in range(nx)],
        lambda: copies.copy(row_slot, row_part, row_land, "core", 1),
    ))
    leading = [
        Job(("query", offset), 2.5, (), functools.partial(query_plane, offset))
        for offset in offsets(nx)[::-1]
    ]
    jobs = [
        Job(("theirs", x), 0.7, (), functools.partial(row_step, 1 - core, row_part, x)) for x in range(nx)
    ] + [
        Job(("ours", x), 0.7, (), functools.partial(row_step, core, row_grad_ref, x)) for x in range(nx)
    ] + [Job("sum", 0.5, ["row", ("ours", nx - 1)], row_sum)]
    sent += play(messages, jobs, leading)
    for piece in range(6):
        query_grad_ref[:, piece * LANES : (piece + 1) * LANES] = total[
            piece // 2, piece % 2, at["x"], at["y"], at["z"]
        ]
    for copy in sent:
        copy.wait_send()


def exchange_step(queries, label_rows, lane_ids, sizes):
    nx, ny, nz = (sizes[axis] for axis in "xyz")
    width, depth = label_rows.shape
    lanes = nz * 16
    f32, bf16 = jnp.float32, jnp.bfloat16
    landings = []
    for first, second, third in ORDERS:
        n1, n2, n3 = sizes[first], sizes[second], sizes[third]
        landings += [
            pltpu.VMEM((n2, 2, n1 // 2, 2, n3, 16, LANES), f32),
            pltpu.VMEM((2, n2 // 2, 2, n3, 16, LANES), f32),
            pltpu.VMEM((n3 - 1, 2, 16, LANES), f32),
        ]
    most = max(sizes.values())
    dma = pltpu.SemaphoreType.DMA
    vmem = pl.BlockSpec(memory_space=pltpu.VMEM)
    return pl.pallas_call(
        functools.partial(kernel, sizes),
        out_shape=(
            jax.ShapeDtypeStruct((width, depth), f32),
            jax.ShapeDtypeStruct((16, depth), f32),
            jax.ShapeDtypeStruct((8, lanes), f32),
        ),
        in_specs=[vmem] * 3,
        out_specs=(vmem,) * 3,
        scratch_shapes=[
            pltpu.VMEM((2, width, depth), bf16),
            pltpu.VMEM((3, 2, nx, ny, nz, 16, LANES), bf16),
            pltpu.VMEM((nx, ny, 2, width, lanes), f32),
            pltpu.VMEM((nx, ny, 2, width, lanes), bf16),
            pltpu.VMEM((3, 2, nx, ny, nz, 16, LANES), f32),
            *landings,
            pltpu.VMEM((nz - 1, 8, lanes), jnp.int32),
            pltpu.VMEM((nx, ny, 8, lanes), jnp.int32),
            pltpu.VMEM((8, lanes), jnp.int32),
            pltpu.VMEM((ny, 8, lanes), jnp.int32),
            pltpu.VMEM((3, 2, nx, ny, lanes), f32),
            pltpu.VMEM((nx - 1, 2, nx, ny, lanes), f32),
            pltpu.VMEM((ny - 1, 2, nx, ny, lanes), f32),
            pltpu.VMEM((nz - 1, 2, nx, ny, lanes), f32),
            pltpu.VMEM((nx, ny, lanes), f32),
            pltpu.VMEM((nx, ny, lanes), f32),
            pltpu.VMEM((width, depth), f32),
            pltpu.VMEM((width, depth), f32),
            dma((COPIES,)), dma((COPIES,)),
            dma((3, most)), dma((3, most)),
        ],
        compiler_params=pltpu.CompilerParams(
            collective_id=0, has_side_effects=True, vmem_limit_bytes=46 << 20
        ),
        name="classifier_step",
    )(queries, label_rows, lane_ids)


def adam_update(label_rows, first_moment, second_moment, row_grad):
    new_first = 0.9 * first_moment + 0.1 * row_grad
    new_second = 0.999 * second_moment + 0.001 * row_grad * row_grad
    update = new_first / (1.0 - 0.9**10) / (jnp.sqrt(new_second / (1.0 - 0.999**10)) + 1e-08)
    return (label_rows - 0.001 * update, new_first, new_second)


def shards(sizes, queries, label_rows, first_moment, second_moment, positive_ids, positive_counts):
    slots = jnp.arange(positive_ids.shape[1], dtype=jnp.int32)
    valid = jnp.where(slots[None, :] < positive_counts[:, None], positive_ids, -1)
    lane_ids = jnp.tile(valid.T, (1, sizes["z"]))
    row_grad, query_grad, logs = exchange_step(queries, label_rows, lane_ids, sizes)
    z = lax.rem(lax.axis_index("inner") // 2, sizes["z"])
    own_total = lax.dynamic_slice_in_dim(logs[0], z * 16, 16, 0)
    new_rows, new_first, new_second = adam_update(label_rows, first_moment, second_moment, row_grad)
    return (new_rows, new_first, new_second, query_grad, own_total)


def solution(mesh):
    sizes = {"x": X, "y": mesh.shape["outer"], "z": Z}
    rows = P(("inner", "outer"), None)
    return jax.shard_map(
        functools.partial(shards, sizes),
        mesh=mesh,
        in_specs=(rows, rows, rows, rows, rows, P(("inner", "outer"))),
        out_specs=(rows, rows, rows, rows, P(("inner", "outer"))),
        check_vma=False,
    )
```

```python
import functools
import itertools

import jax
import jax.numpy as jnp
from jax import lax
from jax.experimental import pallas as pl
from jax.experimental.pallas import tpu as pltpu
from jax.sharding import PartitionSpec as P

X, Z = 4, 8
LANES = 128
MESH = pl.DeviceIdType.MESH
ORDERS = ("xyz", "yxz", "zxy")
GATHER_ORDERS = ("zyx", "zxy", "yxz")
LINK_RATE = 46.0
COPIES = 320


class Place:
    def __init__(self, sizes):
        self.sizes = sizes
        inner = lax.axis_index("inner")
        self.core = lax.rem(inner, 2)
        self.at = {
            "x": inner // (2 * sizes["z"]),
            "z": lax.rem(inner // 2, sizes["z"]),
            "y": lax.axis_index("outer"),
        }

    def ring(self, axis, delta):
        n = self.sizes[axis]
        return lax.rem(self.at[axis] + delta % n, n)

    def link(self, axis, delta):
        return (axis, 0 < delta % self.sizes[axis] <= self.sizes[axis] // 2)

    def device(self, axis, delta):
        at = dict(self.at)
        core = self.core
        if axis == "core":
            core = 1 - core
        else:
            at[axis] = self.ring(axis, delta)
        return ((at["x"] * self.sizes["z"] + at["z"]) * 2 + core, at["y"])


def slab(ref, half, fixed):
    whole = slice(None)
    first = whole if half is None else half
    return ref.at[(first, *(fixed.get(axis, whole) for axis in "xyz"))]


def offsets(n):
    half = n // 2
    return [0, *(sign * d for d in range(1, half) for sign in (1, -1)), half]


def offset_of(n, offset):
    return n // 2 if offset == -(n // 2) else offset


class Message:
    def __init__(self, key, link, kib, hops, deps, copy, landed=None, arrive=None, needs=()):
        self.key, self.link, self.kib, self.hops, self.deps = key, link, kib, hops, set(deps)
        self.needs = set(needs)
        self.copy, self.landed, self.arrive = copy, landed or copy, arrive


class Job:
    def __init__(self, key, cost, deps, work, rank=0):
        self.key, self.cost, self.deps, self.work, self.rank = key, cost, set(deps), work, rank


def play(messages, jobs):
    now, free, arrivals, done, sent = 0.0, {}, [], set(), []
    waiting, jobs = list(messages), list(jobs)

    def start_ready():
        for message in list(waiting):
            if message.deps <= done:
                waiting.remove(message)
                copy = message.copy()
                copy.start()
                sent.append(copy)
                begin = max(now, free.get(message.link, 0.0))
                free[message.link] = begin + message.kib * (message.hops if message.hops < 3 else 1.5) / LINK_RATE
                arrivals.append((free[message.link] + 1.4 + 0.6 * message.hops, len(sent), message))

    def run(job):
        nonlocal now
        job.work()
        now += job.cost
        done.add(job.key)

    start_ready()
    while arrivals or jobs:
        landing = sorted(entry for entry in arrivals if entry[2].needs <= done)
        gap = landing[0][0] - now if landing else 1e9
        ready = [job for job in jobs if job.deps <= done and gap > (-1e9, 0.0, 0.6 * job.cost)[job.rank]]
        if ready:
            job = min(ready, key=lambda job: job.rank)
            jobs.remove(job)
            run(job)
        else:
            arrivals.remove(landing[0])
            when, _, message = landing[0]
            now = max(now, when) + 0.05
            message.landed().wait_recv()
            if message.arrive is not None:
                message.arrive()
                now += message.kib / 2000
            done.add(message.key)
        start_ready()
    assert not waiting
    return sent


class Copies:
    def __init__(self, place, send, recv):
        self.place, self.send, self.recv, self.used = place, send, recv, 0

    def slot(self):
        self.used += 1
        return self.used - 1

    def copy(self, slot, source, target, axis, delta):
        return pltpu.make_async_remote_copy(
            src_ref=source, dst_ref=target, send_sem=self.send.at[slot], recv_sem=self.recv.at[slot],
            device_id=self.place.device(axis, delta), device_id_type=MESH,
        )


def reaches(key, offset, n):
    if key == "rows":
        return True
    if key[0] != "in":
        return False
    _, part, phase, *rest = key
    order = GATHER_ORDERS[part]
    if phase < 3:
        return True
    if order[2] == "x":
        _, way, step = rest
        return offset_of(n, step if way else -step) == offset
    return order[1] != "x" or rest[0] == offset


def gather_messages(copies, part, held):
    place = copies.place
    held = held.at[part]
    first, second, third = GATHER_ORDERS[part]
    at, sizes = place.at, place.sizes
    out = []

    def add(key, axis, delta, kib, hops, deps, block_from):
        slot = copies.slot()
        make = lambda back: copies.copy(slot, block_from(back), block_from(back), axis, delta)
        out.append(Message(
            key, place.link(axis, delta), kib, hops, deps,
            functools.partial(make, 0), functools.partial(make, 1),
        ))

    base = 16 * 2 * LANES * 2 / 1024
    for delta in range(1, sizes[first]):
        far = min(delta, sizes[first] - delta)

        def block(back, delta=delta):
            fixed = dict(at)
            fixed[first] = place.ring(first, -delta * back)
            return slab(held, None, fixed)

        add(("in", part, 1, delta), first, delta, base, far, (), block)
    start = [("in", part, 1, delta) for delta in range(1, sizes[first])]
    base *= sizes[first]
    reach = sizes[second] // 2
    for step in range(1, reach + 1):
        for way, sign in enumerate((1, -1)):

            def block(back, step=step, way=way, sign=sign):
                fixed = {third: at[third], second: place.ring(second, -sign * (step - 1 + back))}
                return slab(held, way if step == reach else None, fixed)

            deps = start if step == 1 else [("in", part, 2, way, step - 1)]
            add(("in", part, 2, way, step), second, sign, base / (1 + (step == reach)), 1, deps, block)
    far = sizes[third] // 2
    for offset in offsets(sizes[second]):
        for step in range(1, far + 1):
            for way, sign in enumerate((1, -1)):

                def block(back, offset=offset, step=step, way=way, sign=sign):
                    fixed = {
                        second: place.ring(second, offset),
                        third: place.ring(third, -sign * (step - 1 + back)),
                    }
                    return slab(held, way if step == far else None, fixed)

                if step > 1:
                    deps = [("in", part, 3, offset, way, step - 1)]
                elif offset == 0:
                    deps = start
                elif abs(offset) == reach:
                    deps = [("in", part, 2, 0, reach), ("in", part, 2, 1, reach)]
                else:
                    deps = [("in", part, 2, 0 if offset < 0 else 1, abs(offset))]
                add(("in", part, 3, offset, way, step), third, sign, base / (1 + (step == far)), 1, deps, block)
    return out


def reduce_messages(copies, part, total, landings):
    place = copies.place
    total = total.at[part]
    first, second, third = ORDERS[part]
    at, sizes = place.at, place.sizes
    out = []

    def add(key, axis, delta, kib, hops, deps, source, landed, mine, needs=()):
        slot = copies.slot()

        def arrive():
            mine()[...] += landed[...]

        out.append(Message(
            key, place.link(axis, delta), kib, hops, deps,
            lambda: copies.copy(slot, source(), landed, axis, delta), None, arrive, needs,
        ))

    base = sizes[third] * 16 * 2 * LANES * 4 / 1024
    reach, far = sizes[first] // 2, sizes[second] // 2
    for number, offset in enumerate(offsets(sizes[second])[::-1]):
        for step in range(1, reach + 1):
            for way, sign in enumerate((1, -1)):

                def block(ahead, offset=offset, step=step, way=way, sign=sign):
                    fixed = {
                        second: place.ring(second, offset),
                        first: place.ring(first, sign * (reach - step + ahead)),
                    }
                    return slab(total, way if step == 1 else None, fixed)

                landed = landings[0].at[number, way, step - 1]
                if step == 1:
                    landed = landed.at[0]
                deps = [("out", part, 1, offset, way, step - 1)] if step > 1 else []
                ahead, here = (
                    [offset_of(sizes["x"], sign * (reach - step + k)) for k in (1, 0)] if first == "x" else [offset] * 2
                )
                deps += [("query", ahead)]
                add(("out", part, 1, offset, way, step), first, sign, base / (1 + (step == 1)), 1, deps,
                    functools.partial(block, 1), landed, functools.partial(block, 0), [("query", here)])
    for step in range(1, far + 1):
        for way, sign in enumerate((1, -1)):

            def block(ahead, step=step, way=way, sign=sign):
                fixed = {first: at[first], second: place.ring(second, sign * (far - step + ahead))}
                return slab(total, way if step == 1 else None, fixed)

            landed = landings[1].at[way, step - 1]
            if step == 1:
                landed = landed.at[0]
            offset = offset_of(sizes[second], sign * (far - step + 1))
            deps = [("out", part, 1, offset, w, reach) for w in range(2)]
            if step > 1:
                deps.append(("out", part, 2, way, step - 1))
            add(("out", part, 2, way, step), second, sign, base / (1 + (step == 1)), 1, deps,
                functools.partial(block, 1), landed, functools.partial(block, 0))
    base /= sizes[third]
    deps = [("out", part, 1, 0, w, reach) for w in range(2)] + [("out", part, 2, w, far) for w in range(2)]
    for delta in range(1, sizes[third]):

        def block(ahead, delta=delta):
            fixed = dict(at)
            fixed[third] = place.ring(third, delta * ahead)
            return slab(total, None, fixed)

        add(("out", part, 3, delta), third, delta, base, min(delta, sizes[third] - delta), deps,
            functools.partial(block, 1), landings[2].at[delta - 1], functools.partial(block, 0))
    return out


def kernel(
    sizes, q_ref, rows_ref, ids_ref, count_ref, row_grad_ref, query_grad_ref, log_ref,
    rows_bf, held, scores, grads, total, *rest,
):
    landings, rest = rest[:9], rest[9:]
    (own, rows, ids_in, count_in, ids_z, ids_x, ids_own, ids_ys, stat, stat_x, stat_y, stat_z, logs, factor, row_part, row_land,
     send, recv, load) = rest
    place = Place(sizes)
    nx, ny, nz = sizes["x"], sizes["y"], sizes["z"]
    width = rows_ref.shape[0]
    lanes = nz * 16
    loading = [
        pltpu.make_async_copy(source, target, load.at[k])
        for k, (source, target) in enumerate(
            ((rows_ref, rows), (q_ref, own), (ids_ref, ids_in), (count_ref, count_in))
        )
    ]
    for copy in loading:
        copy.start()
    at = place.at
    core = place.core

    barrier = pltpu.get_barrier_semaphore()
    peers = [("core", 1)] + [(axis, delta) for axis in "xyz" for delta in range(1, sizes[axis])]
    for axis, delta in peers:
        pl.semaphore_signal(barrier, inc=1, device_id=place.device(axis, delta), device_id_type=MESH)

    for copy in loading[1:]:
        copy.wait()
    for piece in range(6):
        held[piece // 2, piece % 2, at["x"], at["y"], at["z"]] = own[:, piece * LANES : (piece + 1) * LANES]
    lane = lax.broadcasted_iota(jnp.int32, (8, lanes), 1)
    valid = lax.broadcasted_iota(jnp.int32, (8, 16), 0) < count_in[...]
    own_ids = jnp.where(valid, ids_in[...], -1)
    ids_own[...] = jnp.where(lane // 16 == at["z"], jnp.concatenate([own_ids] * nz, axis=1), -1)
    loading[0].wait()
    rows_bf[core] = rows[...].astype(jnp.bfloat16)

    pl.semaphore_wait(barrier, len(peers))

    copies = Copies(place, send, recv)

    def merge_ids():
        merged = ids_own[...]
        for slot in range(nz - 1):
            merged = jnp.maximum(merged, ids_z[slot])
        ids_ys[at["y"]] = merged

    def spread_ids():
        ids_x[at["x"]] = ids_ys[...]

    def count_hits(x, y):
        ids = ids_x[x, y]
        start = ((at["x"] * nz + at["z"]) * 2 * ny + at["y"]) * width

        def step(side, carry):
            label = start + side * (ny * width) + lax.broadcasted_iota(jnp.int32, (width, lanes), 0)
            hits = jnp.zeros((width, lanes), jnp.float32)
            for slot in range(8):
                hits += jnp.where(ids[slot : slot + 1] == label, 1.0, 0.0)
            grads[x, y, side] = hits.astype(jnp.bfloat16)
            return carry

        lax.fori_loop(0, 2, step, 0)

    def id_message(kind, axis, delta, kib, source, target, deps):
        slot = copies.slot()
        return Message(
            (kind, delta), place.link(axis, delta), kib, min(delta, sizes[axis] - delta), deps,
            lambda: copies.copy(slot, source, target(0), axis, delta),
            lambda: copies.copy(slot, source, target(1), axis, delta),
        )

    messages = [
        id_message("ids1", "z", delta, 4, ids_own, lambda back, delta=delta: ids_z.at[delta - 1], ())
        for delta in range(1, nz)
    ]
    messages += [
        id_message("ids2", "y", delta, 4, ids_ys.at[at["y"]],
                   lambda back, delta=delta: ids_ys.at[place.ring("y", -delta * back)], ["merge"])
        for delta in range(1, ny)
    ]
    messages += [
        id_message("ids3", "x", delta, 16, ids_x.at[at["x"]],
                   lambda back, delta=delta: ids_x.at[place.ring("x", -delta * back)], ["spread"])
        for delta in range(1, nx)
    ]
    parts = [gather_messages(copies, part, held) for part in range(3)]
    messages += [m for group in itertools.zip_longest(*parts) for m in group if m is not None]
    rows_slot = copies.slot()

    def rows_copy():
        return copies.copy(rows_slot, rows_bf.at[core], rows_bf.at[core], "core", 1)

    def rows_landed():
        return copies.copy(rows_slot, rows_bf.at[1 - core], rows_bf.at[1 - core], "core", 1)

    messages.append(Message("rows", ("core", True), width * 1.5 / 4, 1, (), rows_copy, rows_landed))
    jobs = [
        Job("merge", 0, [("ids1", delta) for delta in range(1, nz)], merge_ids),
        Job("spread", 0, ["merge", *(("ids2", delta) for delta in range(1, ny))], spread_ids),
        *(
            Job(("hits", x, y), 0.4, ["spread", *(("ids3", delta) for delta in range(1, nx))],
                functools.partial(count_hits, x, y), 2)
            for x in range(nx) for y in range(ny)
        ),
    ]
    def queries_of(x, y, count):
        pieces = [held[p // 2, p % 2, x, pl.ds(y, count)].reshape(count * lanes, LANES) for p in range(6)]
        return jnp.concatenate(pieces, axis=1)

    def score_plane(offset):
        x = place.ring("x", offset)
        for y in range(0, ny, 2):
            query = queries_of(x, y, 2)
            tops = []
            for side in range(2):
                block = lax.dot_general(
                    rows_bf[side], query, (((1,), (1,)), ((), ())), preferred_element_type=jnp.float32
                )
                tops.append(jnp.max(block, axis=0, keepdims=True))
                for k in range(2):
                    scores[x, y + k, side] = block[:, k * lanes : (k + 1) * lanes]
            top = jnp.maximum(tops[0], tops[1])
            for k in range(2):
                part = top[:, k * lanes : (k + 1) * lanes]
                amount = jnp.zeros((1, lanes), jnp.float32)
                for side in range(2):
                    power = jnp.exp(scores[x, y + k, side] - part)
                    scores[x, y + k, side] = power
                    amount += jnp.sum(power, axis=0, keepdims=True)
                stat[0, x, 0, y + k : y + k + 1] = part
                stat[0, x, 1, y + k : y + k + 1] = amount

    rings = (("z", stat_z), ("y", stat_y), ("x", stat_x))

    def combine(stage, offset):
        x = slice(None) if offset is None else place.ring("x", offset)
        slots = rings[stage][1]
        count = sizes[rings[stage][0]] - 1
        top = stat[stage, x, 0]
        for slot in range(count):
            top = jnp.maximum(top, slots[slot, x, 0])
        amount = stat[stage, x, 1] * jnp.exp(stat[stage, x, 0] - top)
        for slot in range(count):
            amount += slots[slot, x, 1] * jnp.exp(slots[slot, x, 0] - top)
        if stage < 2:
            stat[stage + 1, x, 0] = top
            stat[stage + 1, x, 1] = amount
        else:
            log_total = top + jnp.log(amount)
            logs[x] = log_total
            factor[x] = jnp.exp(stat[0, x, 0] - log_total)

    def stat_message(stage, offset, delta, deps):
        slot = copies.slot()
        axis, slots = rings[stage]

        def copy():
            x = slice(None) if offset is None else place.ring("x", offset)
            return copies.copy(slot, stat.at[stage, x], slots.at[delta - 1, x], axis, delta)

        return Message(
            ("stat", stage, offset, delta), place.link(axis, delta), 4, min(delta, sizes[axis] - delta), deps, copy
        )

    order = offsets(nx)
    for offset in order:
        deps = [m.key for m in messages if reaches(m.key, offset, sizes["x"])]
        jobs.append(Job(("score", offset), 1.3, deps, functools.partial(score_plane, offset), 1))
    for stage, (axis, _) in enumerate(rings):
        deltas = range(1, sizes[axis])
        for offset in order if stage < 2 else [None]:
            if stage == 0:
                deps = [("score", offset)]
            elif stage == 1:
                deps = [("combine", 0, offset)]
            else:
                deps = [("combine", 1, offset) for offset in order]
            messages += [stat_message(stage, offset, delta, deps) for delta in deltas]
            jobs.append(Job(
                ("combine", stage, offset), 0.2, [("stat", stage, offset, delta) for delta in deltas],
                functools.partial(combine, stage, offset),
            ))

    order = order[::-1]

    def query_plane(offset):
        x = place.ring("x", offset)

        def step(pair, carry):
            y = 2 * pair
            out = None
            for side in range(2):
                for k in range(2):
                    share = 1.0 / jnp.sum((ids_x[x, y + k] >= 0).astype(jnp.float32), axis=0, keepdims=True)
                    scale = factor[x, pl.ds(y + k, 1)]
                    hits = grads[x, y + k, side].astype(jnp.float32)
                    grads[x, y + k, side] = (scores[x, y + k, side] * scale - hits * share).astype(jnp.bfloat16)
                left = jnp.concatenate([grads[x, y, side], grads[x, y + 1, side]], axis=1)
                term = lax.dot_general(
                    left, rows_bf[side], (((0,), (0,)), ((), ())), preferred_element_type=jnp.float32
                )
                out = term if out is None else out + term
            for piece in range(6):
                total[piece // 2, piece % 2, x, pl.ds(y, 2)] = out[
                    :, piece * LANES : (piece + 1) * LANES
                ].reshape(2, nz, 16, LANES)
            return carry

        lax.fori_loop(0, ny // 2, step, 0)

    def row_step(side, out, offset):
        x = place.ring("x", offset)
        left = jnp.concatenate([grads[x, y, side] for y in range(ny)], axis=1)
        term = jnp.dot(left, queries_of(x, 0, ny), preferred_element_type=jnp.float32)
        if offset == order[0]:
            out[...] = term
        else:
            out[...] += term

    def row_sum():
        row_grad_ref[...] += row_land[...]

    parts = [
        reduce_messages(copies, part, total, landings[3 * part : 3 * part + 3]) for part in range(3)
    ]
    messages += [m for group in itertools.zip_longest(*parts) for m in group if m is not None]
    row_slot = copies.slot()
    messages.append(Message(
        "row", ("core", True), width * 3 / 4, 1, [("theirs", order[-1])],
        lambda: copies.copy(row_slot, row_part, row_land, "core", 1),
    ))
    every_hit = [("hits", x, y) for x in range(nx) for y in range(ny)]
    jobs += [
        Job(("query", offset), 3.0, [("combine", 2, None), *every_hit], functools.partial(query_plane, offset), 1)
        for offset in order
    ]
    for name, side, out in (("theirs", 1 - core, row_part), ("ours", core, row_grad_ref)):
        before = []
        for offset in order:
            jobs.append(Job(
                (name, offset), 0.7, [("query", offset), *before], functools.partial(row_step, side, out, offset), 2
            ))
            before = [(name, offset)]
    jobs.append(Job("sum", 0.5, ["row", ("ours", order[-1])], row_sum, 2))
    sent = play(messages, jobs)
    log_ref[...] = jnp.broadcast_to(logs[at["x"], pl.ds(at["y"], 1)], (8, lanes))
    for piece in range(6):
        query_grad_ref[:, piece * LANES : (piece + 1) * LANES] = total[
            piece // 2, piece % 2, at["x"], at["y"], at["z"]
        ]
    for copy in sent:
        copy.wait_send()


def exchange_step(queries, label_rows, slot_ids, counts, sizes):
    nx, ny, nz = (sizes[axis] for axis in "xyz")
    width, depth = label_rows.shape
    lanes = nz * 16
    f32, bf16 = jnp.float32, jnp.bfloat16
    landings = []
    for first, second, third in ORDERS:
        n1, n2, n3 = sizes[first], sizes[second], sizes[third]
        landings += [
            pltpu.VMEM((n2, 2, n1 // 2, 2, n3, 16, LANES), f32),
            pltpu.VMEM((2, n2 // 2, 2, n3, 16, LANES), f32),
            pltpu.VMEM((n3 - 1, 2, 16, LANES), f32),
        ]
    dma = pltpu.SemaphoreType.DMA
    vmem = pl.BlockSpec(memory_space=pltpu.VMEM)
    return pl.pallas_call(
        functools.partial(kernel, sizes),
        out_shape=(
            jax.ShapeDtypeStruct((width, depth), f32),
            jax.ShapeDtypeStruct((16, depth), f32),
            jax.ShapeDtypeStruct((8, lanes), f32),
        ),
        in_specs=[pl.BlockSpec(memory_space=pltpu.HBM)] * 4,
        out_specs=(vmem,) * 3,
        scratch_shapes=[
            pltpu.VMEM((2, width, depth), bf16),
            pltpu.VMEM((3, 2, nx, ny, nz, 16, LANES), bf16),
            pltpu.VMEM((nx, ny, 2, width, lanes), f32),
            pltpu.VMEM((nx, ny, 2, width, lanes), bf16),
            pltpu.VMEM((3, 2, nx, ny, nz, 16, LANES), f32),
            *landings,
            pltpu.VMEM((16, depth), bf16),
            pltpu.VMEM((width, depth), f32),
            pltpu.VMEM((8, 16), jnp.int32),
            pltpu.VMEM((1, 16), jnp.int32),
            pltpu.VMEM((nz - 1, 8, lanes), jnp.int32),
            pltpu.VMEM((nx, ny, 8, lanes), jnp.int32),
            pltpu.VMEM((8, lanes), jnp.int32),
            pltpu.VMEM((ny, 8, lanes), jnp.int32),
            pltpu.VMEM((3, nx, 2, ny, lanes), f32),
            pltpu.VMEM((nx - 1, nx, 2, ny, lanes), f32),
            pltpu.VMEM((ny - 1, nx, 2, ny, lanes), f32),
            pltpu.VMEM((nz - 1, nx, 2, ny, lanes), f32),
            pltpu.VMEM((nx, ny, lanes), f32),
            pltpu.VMEM((nx, ny, lanes), f32),
            pltpu.VMEM((width, depth), f32),
            pltpu.VMEM((width, depth), f32),
            dma((COPIES,)), dma((COPIES,)), dma((4,)),
        ],
        compiler_params=pltpu.CompilerParams(
            collective_id=0, has_side_effects=True, vmem_limit_bytes=46 << 20
        ),
        name="classifier_step",
    )(queries, label_rows, slot_ids, counts)


def adam_update(label_rows, first_moment, second_moment, row_grad):
    new_first = 0.9 * first_moment + 0.1 * row_grad
    new_second = 0.999 * second_moment + 0.001 * row_grad * row_grad
    update = new_first / (1.0 - 0.9**10) / (jnp.sqrt(new_second / (1.0 - 0.999**10)) + 1e-08)
    return (label_rows - 0.001 * update, new_first, new_second)


def shards(sizes, queries, label_rows, first_moment, second_moment, positive_ids, positive_counts):
    row_grad, query_grad, logs = exchange_step(
        queries, label_rows, positive_ids.T, positive_counts.reshape(1, -1), sizes
    )
    z = lax.rem(lax.axis_index("inner") // 2, sizes["z"])
    own_total = lax.dynamic_slice_in_dim(logs[0], z * 16, 16, 0)
    new_rows, new_first, new_second = adam_update(label_rows, first_moment, second_moment, row_grad)
    return (new_rows, new_first, new_second, query_grad, own_total)


def solution(mesh):
    sizes = {"x": X, "y": mesh.shape["outer"], "z": Z}
    rows = P(("inner", "outer"), None)
    return jax.shard_map(
        functools.partial(shards, sizes),
        mesh=mesh,
        in_specs=(rows, rows, rows, rows, rows, P(("inner", "outer"))),
        out_specs=(rows, rows, rows, rows, P(("inner", "outer"))),
        check_vma=False,
    )
```

```python
import functools
import itertools

import jax
import jax.numpy as jnp
from jax import lax
from jax.experimental import pallas as pl
from jax.experimental.pallas import tpu as pltpu
from jax.sharding import PartitionSpec as P

X, Z = 4, 8
LANES = 128
MESH = pl.DeviceIdType.MESH
ORDERS = ("xyz", "yxz", "zxy")
GATHER_ORDERS = ("zyx", "zxy", "yxz")
LINK_RATE = 46.0
COPIES = 320
ADAM_TILES = 4
ADAM_AHEAD = 4


class Place:
    def __init__(self, sizes):
        self.sizes = sizes
        inner = lax.axis_index("inner")
        self.core = lax.rem(inner, 2)
        self.at = {
            "x": inner // (2 * sizes["z"]),
            "z": lax.rem(inner // 2, sizes["z"]),
            "y": lax.axis_index("outer"),
        }

    def ring(self, axis, delta):
        n = self.sizes[axis]
        return lax.rem(self.at[axis] + delta % n, n)

    def link(self, axis, delta):
        return (axis, 0 < delta % self.sizes[axis] <= self.sizes[axis] // 2)

    def device(self, axis, delta):
        at = dict(self.at)
        core = self.core
        if axis == "core":
            core = 1 - core
        else:
            at[axis] = self.ring(axis, delta)
        return ((at["x"] * self.sizes["z"] + at["z"]) * 2 + core, at["y"])


def slab(ref, half, fixed):
    whole = slice(None)
    first = whole if half is None else half
    return ref.at[(first, *(fixed.get(axis, whole) for axis in "xyz"))]


def offsets(n):
    half = n // 2
    return [0, *(sign * d for d in range(1, half) for sign in (1, -1)), half]


def offset_of(n, offset):
    return n // 2 if offset == -(n // 2) else offset


class Message:
    def __init__(self, key, link, kib, hops, deps, copy, landed=None, arrive=None, needs=()):
        self.key, self.link, self.kib, self.hops, self.deps = key, link, kib, hops, set(deps)
        self.needs = set(needs)
        self.copy, self.landed, self.arrive = copy, landed or copy, arrive


class Job:
    def __init__(self, key, cost, deps, work, rank=0):
        self.key, self.cost, self.deps, self.work, self.rank = key, cost, set(deps), work, rank


def play(messages, jobs):
    now, free, arrivals, done, sent = 0.0, {}, [], set(), []
    waiting, jobs = list(messages), list(jobs)

    def start_ready():
        for message in list(waiting):
            if message.deps <= done:
                waiting.remove(message)
                copy = message.copy()
                copy.start()
                sent.append(copy)
                begin = max(now, free.get(message.link, 0.0))
                free[message.link] = begin + message.kib * (message.hops if message.hops < 3 else 1.5) / LINK_RATE
                arrivals.append((free[message.link] + 1.8 + 0.6 * message.hops, len(sent), message))

    def run(job):
        nonlocal now
        job.work()
        now += job.cost
        done.add(job.key)

    start_ready()
    while arrivals or jobs:
        landing = sorted(entry for entry in arrivals if entry[2].needs <= done)
        gap = landing[0][0] - now if landing else 1e9
        ready = [job for job in jobs if job.deps <= done and gap > (-1e9, 0.0, 0.6 * job.cost)[job.rank]]
        if ready:
            job = min(ready, key=lambda job: job.rank)
            jobs.remove(job)
            run(job)
        else:
            arrivals.remove(landing[0])
            when, _, message = landing[0]
            now = max(now, when) + 0.05
            message.landed().wait_recv()
            if message.arrive is not None:
                message.arrive()
                now += message.kib / 2000
            done.add(message.key)
        start_ready()
    assert not waiting
    return sent


class Copies:
    def __init__(self, place, send, recv):
        self.place, self.send, self.recv, self.used = place, send, recv, 0

    def slot(self):
        self.used += 1
        return self.used - 1

    def copy(self, slot, source, target, axis, delta):
        return pltpu.make_async_remote_copy(
            src_ref=source, dst_ref=target, send_sem=self.send.at[slot], recv_sem=self.recv.at[slot],
            device_id=self.place.device(axis, delta), device_id_type=MESH,
        )


def reaches(key, offset, n):
    if key == "rows":
        return True
    if key[0] != "in":
        return False
    _, part, phase, *rest = key
    order = GATHER_ORDERS[part]
    if phase < 3:
        return True
    if order[2] == "x":
        _, way, step = rest
        return offset_of(n, step if way else -step) == offset
    return order[1] != "x" or rest[0] == offset


def gather_messages(copies, part, held):
    place = copies.place
    held = held.at[part]
    first, second, third = GATHER_ORDERS[part]
    at, sizes = place.at, place.sizes
    out = []

    def add(key, axis, delta, kib, hops, deps, block_from):
        slot = copies.slot()
        make = lambda back: copies.copy(slot, block_from(back), block_from(back), axis, delta)
        out.append(Message(
            key, place.link(axis, delta), kib, hops, deps,
            functools.partial(make, 0), functools.partial(make, 1),
        ))

    base = 16 * 2 * LANES * 2 / 1024
    for delta in range(1, sizes[first]):
        far = min(delta, sizes[first] - delta)

        def block(back, delta=delta):
            fixed = dict(at)
            fixed[first] = place.ring(first, -delta * back)
            return slab(held, None, fixed)

        add(("in", part, 1, delta), first, delta, base, far, (), block)
    start = [("in", part, 1, delta) for delta in range(1, sizes[first])]
    base *= sizes[first]
    reach = sizes[second] // 2
    for step in range(1, reach + 1):
        for way, sign in enumerate((1, -1)):

            def block(back, step=step, way=way, sign=sign):
                fixed = {third: at[third], second: place.ring(second, -sign * (step - 1 + back))}
                return slab(held, way if step == reach else None, fixed)

            deps = start if step == 1 else [("in", part, 2, way, step - 1)]
            add(("in", part, 2, way, step), second, sign, base / (1 + (step == reach)), 1, deps, block)
    far = sizes[third] // 2
    for offset in offsets(sizes[second]):
        for step in range(1, far + 1):
            for way, sign in enumerate((1, -1)):

                def block(back, offset=offset, step=step, way=way, sign=sign):
                    fixed = {
                        second: place.ring(second, offset),
                        third: place.ring(third, -sign * (step - 1 + back)),
                    }
                    return slab(held, way if step == far else None, fixed)

                if step > 1:
                    deps = [("in", part, 3, offset, way, step - 1)]
                elif offset == 0:
                    deps = start
                elif abs(offset) == reach:
                    deps = [("in", part, 2, 0, reach), ("in", part, 2, 1, reach)]
                else:
                    deps = [("in", part, 2, 0 if offset < 0 else 1, abs(offset))]
                add(("in", part, 3, offset, way, step), third, sign, base / (1 + (step == far)), 1, deps, block)
    return out


def reduce_messages(copies, part, total, landings):
    place = copies.place
    total = total.at[part]
    first, second, third = ORDERS[part]
    at, sizes = place.at, place.sizes
    out = []

    def add(key, axis, delta, kib, hops, deps, source, landed, mine, needs=()):
        slot = copies.slot()

        def arrive():
            mine()[...] += landed[...]

        out.append(Message(
            key, place.link(axis, delta), kib, hops, deps,
            lambda: copies.copy(slot, source(), landed, axis, delta), None, arrive, needs,
        ))

    base = sizes[third] * 16 * 2 * LANES * 4 / 1024
    reach, far = sizes[first] // 2, sizes[second] // 2
    for number, offset in enumerate(offsets(sizes[second])[::-1]):
        for step in range(1, reach + 1):
            for way, sign in enumerate((1, -1)):

                def block(ahead, offset=offset, step=step, way=way, sign=sign):
                    fixed = {
                        second: place.ring(second, offset),
                        first: place.ring(first, sign * (reach - step + ahead)),
                    }
                    return slab(total, way if step == 1 else None, fixed)

                landed = landings[0].at[number, way, step - 1]
                if step == 1:
                    landed = landed.at[0]
                deps = [("out", part, 1, offset, way, step - 1)] if step > 1 else []
                if first == "x":
                    ahead, here = ([offset_of(sizes["x"], sign * (reach - step + k))] for k in (1, 0))
                else:
                    ahead = here = [offset] if second == "x" else offsets(sizes["x"])
                deps += [("query", plane) for plane in ahead]
                add(("out", part, 1, offset, way, step), first, sign, base / (1 + (step == 1)), 1, deps,
                    functools.partial(block, 1), landed, functools.partial(block, 0),
                    [("query", plane) for plane in here])
    for step in range(1, far + 1):
        for way, sign in enumerate((1, -1)):

            def block(ahead, step=step, way=way, sign=sign):
                fixed = {first: at[first], second: place.ring(second, sign * (far - step + ahead))}
                return slab(total, way if step == 1 else None, fixed)

            landed = landings[1].at[way, step - 1]
            if step == 1:
                landed = landed.at[0]
            offset = offset_of(sizes[second], sign * (far - step + 1))
            deps = [("out", part, 1, offset, w, reach) for w in range(2)]
            if step > 1:
                deps.append(("out", part, 2, way, step - 1))
            add(("out", part, 2, way, step), second, sign, base / (1 + (step == 1)), 1, deps,
                functools.partial(block, 1), landed, functools.partial(block, 0))
    base /= sizes[third]
    deps = [("out", part, 1, 0, w, reach) for w in range(2)] + [("out", part, 2, w, far) for w in range(2)]
    for delta in range(1, sizes[third]):

        def block(ahead, delta=delta):
            fixed = dict(at)
            fixed[third] = place.ring(third, delta * ahead)
            return slab(total, None, fixed)

        add(("out", part, 3, delta), third, delta, base, min(delta, sizes[third] - delta), deps,
            functools.partial(block, 1), landings[2].at[delta - 1], functools.partial(block, 0))
    return out


def kernel(
    sizes, q_ref, rows_ref, ids_ref, count_ref, row_grad_ref, query_grad_ref, log_ref,
    rows_bf, held, scores, grads, total, *rest,
):
    landings, rest = rest[:9], rest[9:]
    (own, rows, ids_in, count_in, ids_z, ids_x, ids_own, ids_ys, stat, stat_x, stat_y, stat_z, logs, factor, row_part, row_land,
     send, recv, load) = rest
    place = Place(sizes)
    nx, ny, nz = sizes["x"], sizes["y"], sizes["z"]
    width = rows_ref.shape[0]
    lanes = nz * 16
    loading = [
        pltpu.make_async_copy(source, target, load.at[k])
        for k, (source, target) in enumerate(
            ((rows_ref, rows), (q_ref, own), (ids_ref, ids_in), (count_ref, count_in))
        )
    ]
    for copy in loading:
        copy.start()
    at = place.at
    core = place.core

    barrier = pltpu.get_barrier_semaphore()
    peers = [("core", 1)] + [(axis, delta) for axis in "xyz" for delta in range(1, sizes[axis])]
    for axis, delta in peers:
        pl.semaphore_signal(barrier, inc=1, device_id=place.device(axis, delta), device_id_type=MESH)

    for copy in loading[1:]:
        copy.wait()
    for piece in range(6):
        held[piece // 2, piece % 2, at["x"], at["y"], at["z"]] = own[:, piece * LANES : (piece + 1) * LANES]
    lane = lax.broadcasted_iota(jnp.int32, (8, lanes), 1)
    valid = lax.broadcasted_iota(jnp.int32, (8, 16), 0) < count_in[...]
    own_ids = jnp.where(valid, ids_in[...], -1)
    ids_own[...] = jnp.where(lane // 16 == at["z"], jnp.concatenate([own_ids] * nz, axis=1), -1)

    def cast_rows():
        loading[0].wait()
        rows_bf[core] = rows[...].astype(jnp.bfloat16)

    pl.semaphore_wait(barrier, len(peers))

    copies = Copies(place, send, recv)

    def merge_ids():
        merged = ids_own[...]
        for slot in range(nz - 1):
            merged = jnp.maximum(merged, ids_z[slot])
        ids_ys[at["y"]] = merged

    def spread_ids():
        ids_x[at["x"]] = ids_ys[...]

    def count_hits(x, y):
        ids = ids_x[x, y]
        start = ((at["x"] * nz + at["z"]) * 2 * ny + at["y"]) * width

        def step(side, carry):
            label = start + side * (ny * width) + lax.broadcasted_iota(jnp.int32, (width, lanes), 0)
            hits = jnp.zeros((width, lanes), jnp.float32)
            for slot in range(8):
                hits += jnp.where(ids[slot : slot + 1] == label, 1.0, 0.0)
            grads[x, y, side] = hits.astype(jnp.bfloat16)
            return carry

        lax.fori_loop(0, 2, step, 0)

    def id_message(kind, axis, delta, kib, source, target, deps):
        slot = copies.slot()
        return Message(
            (kind, delta), place.link(axis, delta), kib, min(delta, sizes[axis] - delta), deps,
            lambda: copies.copy(slot, source, target(0), axis, delta),
            lambda: copies.copy(slot, source, target(1), axis, delta),
        )

    messages = [
        id_message("ids1", "z", delta, 4, ids_own, lambda back, delta=delta: ids_z.at[delta - 1], ())
        for delta in range(1, nz)
    ]
    messages += [
        id_message("ids2", "y", delta, 4, ids_ys.at[at["y"]],
                   lambda back, delta=delta: ids_ys.at[place.ring("y", -delta * back)], ["merge"])
        for delta in range(1, ny)
    ]
    messages += [
        id_message("ids3", "x", delta, 16, ids_x.at[at["x"]],
                   lambda back, delta=delta: ids_x.at[place.ring("x", -delta * back)], ["spread"])
        for delta in range(1, nx)
    ]
    parts = [gather_messages(copies, part, held) for part in range(3)]
    messages += [m for group in itertools.zip_longest(*parts) for m in group if m is not None]
    rows_slot = copies.slot()

    def rows_copy():
        return copies.copy(rows_slot, rows_bf.at[core], rows_bf.at[core], "core", 1)

    def rows_landed():
        return copies.copy(rows_slot, rows_bf.at[1 - core], rows_bf.at[1 - core], "core", 1)

    messages.append(Message("rows", ("core", True), width * 1.5 / 4, 1, ["cast"], rows_copy, rows_landed))
    jobs = [
        Job("cast", 0.6, (), cast_rows, 2),
        Job("merge", 0, [("ids1", delta) for delta in range(1, nz)], merge_ids),
        Job("spread", 0, ["merge", *(("ids2", delta) for delta in range(1, ny))], spread_ids),
        *(
            Job(("hits", x, y), 0.4, ["spread", *(("ids3", delta) for delta in range(1, nx))],
                functools.partial(count_hits, x, y), 2)
            for x in range(nx) for y in range(ny)
        ),
    ]
    def queries_of(x, y, count):
        pieces = [held[p // 2, p % 2, x, pl.ds(y, count)].reshape(count * lanes, LANES) for p in range(6)]
        return jnp.concatenate(pieces, axis=1)

    def score_plane(offset):
        x = place.ring("x", offset)
        for y in range(0, ny, 2):
            query = queries_of(x, y, 2)
            tops = []
            for side in range(2):
                block = lax.dot_general(
                    rows_bf[side], query, (((1,), (1,)), ((), ())), preferred_element_type=jnp.float32
                )
                tops.append(jnp.max(block, axis=0, keepdims=True))
                for k in range(2):
                    scores[x, y + k, side] = block[:, k * lanes : (k + 1) * lanes]
            top = jnp.maximum(tops[0], tops[1])
            for k in range(2):
                part = top[:, k * lanes : (k + 1) * lanes]
                amount = jnp.zeros((1, lanes), jnp.float32)
                for side in range(2):
                    power = jnp.exp(scores[x, y + k, side] - part)
                    scores[x, y + k, side] = power
                    amount += jnp.sum(power, axis=0, keepdims=True)
                stat[0, x, 0, y + k : y + k + 1] = part
                stat[0, x, 1, y + k : y + k + 1] = amount

    rings = (("z", stat_z), ("y", stat_y), ("x", stat_x))

    def combine(stage, offset):
        x = slice(None) if offset is None else place.ring("x", offset)
        slots = rings[stage][1]
        count = sizes[rings[stage][0]] - 1
        top = stat[stage, x, 0]
        for slot in range(count):
            top = jnp.maximum(top, slots[slot, x, 0])
        amount = stat[stage, x, 1] * jnp.exp(stat[stage, x, 0] - top)
        for slot in range(count):
            amount += slots[slot, x, 1] * jnp.exp(slots[slot, x, 0] - top)
        if stage < 2:
            stat[stage + 1, x, 0] = top
            stat[stage + 1, x, 1] = amount
        else:
            log_total = top + jnp.log(amount)
            logs[x] = log_total
            factor[x] = jnp.exp(stat[0, x, 0] - log_total)

    def stat_message(stage, offset, delta, deps):
        slot = copies.slot()
        axis, slots = rings[stage]

        def copy():
            x = slice(None) if offset is None else place.ring("x", offset)
            return copies.copy(slot, stat.at[stage, x], slots.at[delta - 1, x], axis, delta)

        return Message(
            ("stat", stage, offset, delta), place.link(axis, delta), 4, min(delta, sizes[axis] - delta), deps, copy
        )

    order = offsets(nx)
    for offset in order:
        deps = [m.key for m in messages if reaches(m.key, offset, sizes["x"])]
        jobs.append(Job(("score", offset), 1.3, deps, functools.partial(score_plane, offset), 1))
    for stage, (axis, _) in enumerate(rings):
        deltas = range(1, sizes[axis])
        for offset in order if stage < 2 else [None]:
            if stage == 0:
                deps = [("score", offset)]
            elif stage == 1:
                deps = [("combine", 0, offset)]
            else:
                deps = [("combine", 1, offset) for offset in order]
            messages += [stat_message(stage, offset, delta, deps) for delta in deltas]
            jobs.append(Job(
                ("combine", stage, offset), 0.2, [("stat", stage, offset, delta) for delta in deltas],
                functools.partial(combine, stage, offset),
            ))

    order = order[::-1]

    def query_plane(offset):
        x = place.ring("x", offset)

        def step(pair, carry):
            y = 2 * pair
            out = None
            for side in range(2):
                for k in range(2):
                    share = 1.0 / jnp.sum((ids_x[x, y + k] >= 0).astype(jnp.float32), axis=0, keepdims=True)
                    scale = factor[x, pl.ds(y + k, 1)]
                    hits = grads[x, y + k, side].astype(jnp.float32)
                    grads[x, y + k, side] = (scores[x, y + k, side] * scale - hits * share).astype(jnp.bfloat16)
                left = jnp.concatenate([grads[x, y, side], grads[x, y + 1, side]], axis=1)
                term = lax.dot_general(
                    left, rows_bf[side], (((0,), (0,)), ((), ())), preferred_element_type=jnp.float32
                )
                out = term if out is None else out + term
            for piece in range(6):
                total[piece // 2, piece % 2, x, pl.ds(y, 2)] = out[
                    :, piece * LANES : (piece + 1) * LANES
                ].reshape(2, nz, 16, LANES)
            return carry

        lax.fori_loop(0, ny // 2, step, 0)

    def row_step(side, out, offset):
        x = place.ring("x", offset)
        left = jnp.concatenate([grads[x, y, side] for y in range(ny)], axis=1)
        term = jnp.dot(left, queries_of(x, 0, ny), preferred_element_type=jnp.float32)
        if offset == order[0]:
            out[...] = term
        else:
            out[...] += term

    def row_sum():
        row_grad_ref[...] += row_land[...]

    parts = [
        reduce_messages(copies, part, total, landings[3 * part : 3 * part + 3]) for part in range(3)
    ]
    messages += [m for group in itertools.zip_longest(*parts) for m in group if m is not None]
    row_slot = copies.slot()
    messages.append(Message(
        "row", ("core", True), width * 3 / 4, 1, [("theirs", order[-1])],
        lambda: copies.copy(row_slot, row_part, row_land, "core", 1),
    ))
    every_hit = [("hits", x, y) for x in range(nx) for y in range(ny)]
    jobs += [
        Job(("query", offset), 1.6, [("combine", 2, None), *every_hit], functools.partial(query_plane, offset), 1)
        for offset in order
    ]
    for name, side, out in (("theirs", 1 - core, row_part), ("ours", core, row_grad_ref)):
        before = []
        for offset in order:
            jobs.append(Job(
                (name, offset), 0.7, [("query", offset), *before], functools.partial(row_step, side, out, offset), 2
            ))
            before = [(name, offset)]
    jobs.append(Job("sum", 0.5, ["row", ("ours", order[-1])], row_sum, 2))
    sent = play(messages, jobs)
    log_ref[...] = jnp.broadcast_to(logs[at["x"], pl.ds(at["y"], 1)], (8, lanes))
    for piece in range(6):
        query_grad_ref[:, piece * LANES : (piece + 1) * LANES] = total[
            piece // 2, piece % 2, at["x"], at["y"], at["z"]
        ]
    for copy in sent:
        copy.wait_send()


def exchange_step(queries, label_rows, slot_ids, counts, sizes):
    nx, ny, nz = (sizes[axis] for axis in "xyz")
    width, depth = label_rows.shape
    lanes = nz * 16
    f32, bf16 = jnp.float32, jnp.bfloat16
    landings = []
    for first, second, third in ORDERS:
        n1, n2, n3 = sizes[first], sizes[second], sizes[third]
        landings += [
            pltpu.VMEM((n2, 2, n1 // 2, 2, n3, 16, LANES), f32),
            pltpu.VMEM((2, n2 // 2, 2, n3, 16, LANES), f32),
            pltpu.VMEM((n3 - 1, 2, 16, LANES), f32),
        ]
    dma = pltpu.SemaphoreType.DMA
    vmem = pl.BlockSpec(memory_space=pltpu.VMEM)
    return pl.pallas_call(
        functools.partial(kernel, sizes),
        out_shape=(
            jax.ShapeDtypeStruct((width, depth), f32),
            jax.ShapeDtypeStruct((16, depth), f32),
            jax.ShapeDtypeStruct((8, lanes), f32),
        ),
        in_specs=[pl.BlockSpec(memory_space=pltpu.HBM)] * 4,
        out_specs=(vmem,) * 3,
        scratch_shapes=[
            pltpu.VMEM((2, width, depth), bf16),
            pltpu.VMEM((3, 2, nx, ny, nz, 16, LANES), bf16),
            pltpu.VMEM((nx, ny, 2, width, lanes), f32),
            pltpu.VMEM((nx, ny, 2, width, lanes), bf16),
            pltpu.VMEM((3, 2, nx, ny, nz, 16, LANES), f32),
            *landings,
            pltpu.VMEM((16, depth), bf16),
            pltpu.VMEM((width, depth), f32),
            pltpu.VMEM((8, 16), jnp.int32),
            pltpu.VMEM((1, 16), jnp.int32),
            pltpu.VMEM((nz - 1, 8, lanes), jnp.int32),
            pltpu.VMEM((nx, ny, 8, lanes), jnp.int32),
            pltpu.VMEM((8, lanes), jnp.int32),
            pltpu.VMEM((ny, 8, lanes), jnp.int32),
            pltpu.VMEM((3, nx, 2, ny, lanes), f32),
            pltpu.VMEM((nx - 1, nx, 2, ny, lanes), f32),
            pltpu.VMEM((ny - 1, nx, 2, ny, lanes), f32),
            pltpu.VMEM((nz - 1, nx, 2, ny, lanes), f32),
            pltpu.VMEM((nx, ny, lanes), f32),
            pltpu.VMEM((nx, ny, lanes), f32),
            pltpu.VMEM((width, depth), f32),
            pltpu.VMEM((width, depth), f32),
            dma((COPIES,)), dma((COPIES,)), dma((4,)),
        ],
        compiler_params=pltpu.CompilerParams(
            collective_id=0, has_side_effects=True, vmem_limit_bytes=60 << 20
        ),
        name="classifier_step",
    )(queries, label_rows, slot_ids, counts)


def adam_kernel(nz, grad_ref, rows_ref, first_ref, second_ref, query_ref, log_ref,
                new_rows_ref, new_first_ref, new_second_ref, query_grad_ref, own_ref,
                grad, rows, first, second, new_rows, new_first, new_second, load, store):
    count = grad.shape[0] // ADAM_TILES
    loads = []
    for number in range(ADAM_TILES):
        tile = pl.ds(number * count, count)
        pairs = ((grad_ref, grad), (rows_ref, rows), (first_ref, first), (second_ref, second))
        loads.append([
            pltpu.make_async_copy(source.at[tile], target.at[tile], load.at[number, k])
            for k, (source, target) in enumerate(pairs)
        ])
    for copy in itertools.chain(*loads[:ADAM_AHEAD]):
        copy.start()
    query_grad_ref[...] = query_ref[...]
    z = lax.rem(lax.axis_index("inner") // 2, nz)
    own = jnp.zeros((1, 16), jnp.float32)
    for k in range(nz):
        own = jnp.where(z == k, log_ref[0:1, k * 16 : (k + 1) * 16], own)
    own_ref[...] = own
    stores = []
    for number in range(ADAM_TILES):
        tile = pl.ds(number * count, count)
        for copy in itertools.chain(*loads[number + ADAM_AHEAD : number + ADAM_AHEAD + 1]):
            copy.start()
        for copy in loads[number]:
            copy.wait()
        gradient = grad[tile]
        moment = 0.9 * first[tile] + 0.1 * gradient
        spread = 0.999 * second[tile] + 0.001 * gradient * gradient
        update = moment / (1.0 - 0.9**10) / (jnp.sqrt(spread / (1.0 - 0.999**10)) + 1e-08)
        new_rows[tile] = rows[tile] - 0.001 * update
        new_first[tile] = moment
        new_second[tile] = spread
        pairs = ((new_rows, new_rows_ref), (new_first, new_first_ref), (new_second, new_second_ref))
        for k, (source, target) in enumerate(pairs):
            copy = pltpu.make_async_copy(source.at[tile], target.at[tile], store.at[number, k])
            copy.start()
            stores.append(copy)
    for copy in stores:
        copy.wait()


def adam_step(row_grad, label_rows, first_moment, second_moment, query_grad, logs, nz):
    f32 = jnp.float32
    whole = jax.ShapeDtypeStruct(label_rows.shape, f32)
    vmem = pl.BlockSpec(memory_space=pltpu.VMEM)
    hbm = pl.BlockSpec(memory_space=pltpu.HBM)
    return pl.pallas_call(
        functools.partial(adam_kernel, nz),
        out_shape=(whole, whole, whole, jax.ShapeDtypeStruct(query_grad.shape, f32), jax.ShapeDtypeStruct((1, 16), f32)),
        in_specs=[hbm] * 4 + [vmem] * 2,
        out_specs=(hbm, hbm, hbm, vmem, vmem),
        scratch_shapes=[
            *[pltpu.VMEM(label_rows.shape, f32)] * 7,
            pltpu.SemaphoreType.DMA((ADAM_TILES, 4)), pltpu.SemaphoreType.DMA((ADAM_TILES, 3)),
        ],
        compiler_params=pltpu.CompilerParams(vmem_limit_bytes=60 << 20),
        name="adam_step",
    )(row_grad, label_rows, first_moment, second_moment, query_grad, logs)


def shards(sizes, queries, label_rows, first_moment, second_moment, positive_ids, positive_counts):
    row_grad, query_grad, logs = exchange_step(
        queries, label_rows, positive_ids.T, positive_counts.reshape(1, -1), sizes
    )
    new_rows, new_first, new_second, query_grad, own_total = adam_step(
        row_grad, label_rows, first_moment, second_moment, query_grad, logs, sizes["z"]
    )
    return (new_rows, new_first, new_second, query_grad, own_total.reshape(-1))


def solution(mesh):
    sizes = {"x": X, "y": mesh.shape["outer"], "z": Z}
    rows = P(("inner", "outer"), None)
    return jax.shard_map(
        functools.partial(shards, sizes),
        mesh=mesh,
        in_specs=(rows, rows, rows, rows, rows, P(("inner", "outer"))),
        out_specs=(rows, rows, rows, rows, P(("inner", "outer"))),
        check_vma=False,
    )
```

```python
import functools
import itertools

import jax
import jax.numpy as jnp
from jax import lax
from jax.experimental import pallas as pl
from jax.experimental.pallas import tpu as pltpu
from jax.sharding import PartitionSpec as P

X, Z = 4, 8
LANES = 128
MESH = pl.DeviceIdType.MESH
ORDERS = ("xyz", "yxz", "zxy")
GATHER_ORDERS = ("zyx", "zxy", "yxz")
LINK_RATE = 46.0
COPIES = 320
ADAM_TILES = 4
ADAM_AHEAD = 4


class Place:
    def __init__(self, sizes):
        self.sizes = sizes
        inner = lax.axis_index("inner")
        self.core = lax.rem(inner, 2)
        self.at = {
            "x": inner // (2 * sizes["z"]),
            "z": lax.rem(inner // 2, sizes["z"]),
            "y": lax.axis_index("outer"),
        }

    def ring(self, axis, delta):
        n = self.sizes[axis]
        return lax.rem(self.at[axis] + delta % n, n)

    def link(self, axis, delta):
        return (axis, 0 < delta % self.sizes[axis] <= self.sizes[axis] // 2)

    def device(self, axis, delta):
        at = dict(self.at)
        core = self.core
        if axis == "core":
            core = 1 - core
        else:
            at[axis] = self.ring(axis, delta)
        return ((at["x"] * self.sizes["z"] + at["z"]) * 2 + core, at["y"])


def slab(ref, half, fixed):
    whole = slice(None)
    first = whole if half is None else half
    return ref.at[(first, *(fixed.get(axis, whole) for axis in "xyz"))]


def offsets(n):
    half = n // 2
    return [0, *(sign * d for d in range(1, half) for sign in (1, -1)), half]


def offset_of(n, offset):
    offset = (offset + n) % n
    return offset if offset <= n // 2 else offset - n


class Message:
    def __init__(self, key, link, kib, hops, deps, copy, landed=None, arrive=None, needs=()):
        self.key, self.link, self.kib, self.hops, self.deps = key, link, kib, hops, set(deps)
        self.needs = set(needs)
        self.copy, self.landed, self.arrive = copy, landed or copy, arrive


class Job:
    def __init__(self, key, cost, deps, work, rank=0):
        self.key, self.cost, self.deps, self.work, self.rank = key, cost, set(deps), work, rank


def play(messages, jobs):
    now, free, arrivals, done, sent = 0.0, {}, [], set(), []
    waiting, jobs = list(messages), list(jobs)

    def start_ready():
        for message in list(waiting):
            if message.deps <= done:
                waiting.remove(message)
                copy = message.copy()
                copy.start()
                sent.append(copy)
                begin = max(now, free.get(message.link, 0.0))
                free[message.link] = begin + message.kib * (message.hops if message.hops < 3 else 1.5) / LINK_RATE
                arrivals.append((free[message.link] + 2.7 + 0.6 * message.hops, len(sent), message))

    def run(job):
        nonlocal now
        job.work()
        now += job.cost
        done.add(job.key)

    start_ready()
    while arrivals or jobs:
        landing = sorted(entry for entry in arrivals if entry[2].needs <= done)
        gap = landing[0][0] - now if landing else 1e9
        ready = [job for job in jobs if job.deps <= done and gap > (-1e9, 0.0, 0.6 * job.cost)[job.rank]]
        if ready:
            job = min(ready, key=lambda job: job.rank)
            jobs.remove(job)
            run(job)
        else:
            arrivals.remove(landing[0])
            when, _, message = landing[0]
            now = max(now, when) + 0.05
            message.landed().wait_recv()
            if message.arrive is not None:
                message.arrive()
                now += message.kib / 2000
            done.add(message.key)
        start_ready()
    assert not waiting
    return sent


class Copies:
    def __init__(self, place, send, recv):
        self.place, self.send, self.recv, self.used = place, send, recv, 0

    def slot(self):
        self.used += 1
        return self.used - 1

    def copy(self, slot, source, target, axis, delta):
        return pltpu.make_async_remote_copy(
            src_ref=source, dst_ref=target, send_sem=self.send.at[slot], recv_sem=self.recv.at[slot],
            device_id=self.place.device(axis, delta), device_id_type=MESH,
        )


def reaches(key, offset, n):
    if key == "rows":
        return True
    if key[0] != "in":
        return False
    _, part, phase, *rest = key
    order = GATHER_ORDERS[part]
    if phase < 3:
        return True
    if order[2] == "x":
        _, way, step = rest
        return offset_of(n, step if way else -step) == offset
    return order[1] != "x" or rest[0] == offset


def gather_messages(copies, part, held):
    place = copies.place
    held = held.at[part]
    first, second, third = GATHER_ORDERS[part]
    at, sizes = place.at, place.sizes
    out = []

    def add(key, axis, delta, kib, hops, deps, block_from):
        slot = copies.slot()
        make = lambda back: copies.copy(slot, block_from(back), block_from(back), axis, delta)
        out.append(Message(
            key, place.link(axis, delta), kib, hops, deps,
            functools.partial(make, 0), functools.partial(make, 1),
        ))

    base = 16 * 2 * LANES * 2 / 1024
    for delta in range(1, sizes[first]):
        far = min(delta, sizes[first] - delta)

        def block(back, delta=delta):
            fixed = dict(at)
            fixed[first] = place.ring(first, -delta * back)
            return slab(held, None, fixed)

        add(("in", part, 1, delta), first, delta, base, far, (), block)
    start = [("in", part, 1, delta) for delta in range(1, sizes[first])]
    base *= sizes[first]
    for delta in range(1, sizes[second]):

        def block(back, delta=delta):
            return slab(held, None, {third: at[third], second: place.ring(second, -delta * back)})

        add(("in", part, 2, delta), second, delta, base, min(delta, sizes[second] - delta), start, block)
    far = sizes[third] // 2
    for offset in offsets(sizes[second]):
        for step in range(1, far + 1):
            for way, sign in enumerate((1, -1)):

                def block(back, offset=offset, step=step, way=way, sign=sign):
                    fixed = {
                        second: place.ring(second, offset),
                        third: place.ring(third, -sign * (step - 1 + back)),
                    }
                    return slab(held, way if step == far else None, fixed)

                if step > 1:
                    deps = [("in", part, 3, offset, way, step - 1)]
                elif offset == 0:
                    deps = start
                else:
                    deps = [("in", part, 2, -offset % sizes[second])]
                add(("in", part, 3, offset, way, step), third, sign, base / (1 + (step == far)), 1, deps, block)
    return out


def reduce_messages(copies, part, total, landings):
    place = copies.place
    total = total.at[part]
    first, second, third = ORDERS[part]
    at, sizes = place.at, place.sizes
    out = []

    def add(key, axis, delta, kib, hops, deps, source, landed, mine, needs=()):
        slot = copies.slot()

        def arrive():
            mine()[...] += landed[...]

        out.append(Message(
            key, place.link(axis, delta), kib, hops, deps,
            lambda: copies.copy(slot, source(), landed, axis, delta), None, arrive, needs,
        ))

    base = sizes[third] * 16 * 2 * LANES * 4 / 1024
    reach, far = sizes[first] // 2, sizes[second] // 2
    for number, offset in enumerate(offsets(sizes[second])[::-1]):
        for step in range(1, reach + 1):
            for way, sign in enumerate((1, -1)):

                def block(ahead, offset=offset, step=step, way=way, sign=sign):
                    fixed = {
                        second: place.ring(second, offset),
                        first: place.ring(first, sign * (reach - step + ahead)),
                    }
                    return slab(total, way if step == 1 else None, fixed)

                landed = landings[0].at[number, way, step - 1]
                if step == 1:
                    landed = landed.at[0]
                deps = [("out", part, 1, offset, way, step - 1)] if step > 1 else []
                if first == "x":
                    ahead, here = ([offset_of(sizes["x"], sign * (reach - step + k))] for k in (1, 0))
                else:
                    ahead = here = [offset] if second == "x" else offsets(sizes["x"])
                deps += [("query", plane) for plane in ahead]
                add(("out", part, 1, offset, way, step), first, sign, base / (1 + (step == 1)), 1, deps,
                    functools.partial(block, 1), landed, functools.partial(block, 0),
                    [("query", plane) for plane in here])
    for step in range(1, far + 1):
        for way, sign in enumerate((1, -1)):

            def block(ahead, step=step, way=way, sign=sign):
                fixed = {first: at[first], second: place.ring(second, sign * (far - step + ahead))}
                return slab(total, way if step == 1 else None, fixed)

            landed = landings[1].at[way, step - 1]
            if step == 1:
                landed = landed.at[0]
            offset = offset_of(sizes[second], sign * (far - step + 1))
            deps = [("out", part, 1, offset, w, reach) for w in range(2)]
            if step > 1:
                deps.append(("out", part, 2, way, step - 1))
            add(("out", part, 2, way, step), second, sign, base / (1 + (step == 1)), 1, deps,
                functools.partial(block, 1), landed, functools.partial(block, 0))
    base /= sizes[third]
    deps = [("out", part, 1, 0, w, reach) for w in range(2)] + [("out", part, 2, w, far) for w in range(2)]
    for delta in range(1, sizes[third]):

        def block(ahead, delta=delta):
            fixed = dict(at)
            fixed[third] = place.ring(third, delta * ahead)
            return slab(total, None, fixed)

        add(("out", part, 3, delta), third, delta, base, min(delta, sizes[third] - delta), deps,
            functools.partial(block, 1), landings[2].at[delta - 1], functools.partial(block, 0))
    return out


def kernel(
    sizes, q_ref, rows_ref, ids_ref, count_ref, row_grad_ref, query_grad_ref, log_ref,
    rows_bf, held, scores, grads, total, *rest,
):
    landings, rest = rest[:9], rest[9:]
    (own, rows, ids_in, count_in, ids_z, ids_x, ids_own, ids_ys, stat, stat_x, stat_y, stat_z, logs, factor, row_part, row_land,
     send, recv, load) = rest
    place = Place(sizes)
    nx, ny, nz = sizes["x"], sizes["y"], sizes["z"]
    width = rows_ref.shape[0]
    lanes = nz * 16
    loading = [
        pltpu.make_async_copy(source, target, load.at[k])
        for k, (source, target) in enumerate(
            ((rows_ref, rows), (q_ref, own), (ids_ref, ids_in), (count_ref, count_in))
        )
    ]
    for copy in loading:
        copy.start()
    at = place.at
    core = place.core

    barrier = pltpu.get_barrier_semaphore()
    peers = [("core", 1)] + [(axis, delta) for axis in "xyz" for delta in range(1, sizes[axis])]
    for axis, delta in peers:
        pl.semaphore_signal(barrier, inc=1, device_id=place.device(axis, delta), device_id_type=MESH)

    for copy in loading[1:]:
        copy.wait()
    for piece in range(6):
        held[piece // 2, piece % 2, at["x"], at["y"], at["z"]] = own[:, piece * LANES : (piece + 1) * LANES]
    lane = lax.broadcasted_iota(jnp.int32, (8, lanes), 1)
    valid = lax.broadcasted_iota(jnp.int32, (8, 16), 0) < count_in[...]
    own_ids = jnp.where(valid, ids_in[...], -1)
    ids_own[...] = jnp.where(lane // 16 == at["z"], jnp.concatenate([own_ids] * nz, axis=1), -1)

    def cast_rows():
        loading[0].wait()
        rows_bf[core] = rows[...].astype(jnp.bfloat16)

    pl.semaphore_wait(barrier, len(peers))

    copies = Copies(place, send, recv)

    def merge_ids():
        merged = ids_own[...]
        for slot in range(nz - 1):
            merged = jnp.maximum(merged, ids_z[slot])
        ids_ys[at["y"]] = merged

    def spread_ids():
        ids_x[at["x"]] = ids_ys[...]

    def count_hits(x, y):
        ids = ids_x[x, y]
        start = ((at["x"] * nz + at["z"]) * 2 * ny + at["y"]) * width

        def step(side, carry):
            label = start + side * (ny * width) + lax.broadcasted_iota(jnp.int32, (width, lanes), 0)
            hits = jnp.zeros((width, lanes), jnp.float32)
            for slot in range(8):
                hits += jnp.where(ids[slot : slot + 1] == label, 1.0, 0.0)
            grads[x, y, side] = hits.astype(jnp.bfloat16)
            return carry

        lax.fori_loop(0, 2, step, 0)

    def id_message(kind, axis, delta, kib, source, target, deps):
        slot = copies.slot()
        return Message(
            (kind, delta), place.link(axis, delta), kib, min(delta, sizes[axis] - delta), deps,
            lambda: copies.copy(slot, source, target(0), axis, delta),
            lambda: copies.copy(slot, source, target(1), axis, delta),
        )

    messages = [
        id_message("ids1", "z", delta, 4, ids_own, lambda back, delta=delta: ids_z.at[delta - 1], ())
        for delta in range(1, nz)
    ]
    messages += [
        id_message("ids2", "y", delta, 4, ids_ys.at[at["y"]],
                   lambda back, delta=delta: ids_ys.at[place.ring("y", -delta * back)], ["merge"])
        for delta in range(1, ny)
    ]
    messages += [
        id_message("ids3", "x", delta, 16, ids_x.at[at["x"]],
                   lambda back, delta=delta: ids_x.at[place.ring("x", -delta * back)], ["spread"])
        for delta in range(1, nx)
    ]
    parts = [gather_messages(copies, part, held) for part in range(3)]
    messages += [m for group in itertools.zip_longest(*parts) for m in group if m is not None]
    rows_slot = copies.slot()

    def rows_copy():
        return copies.copy(rows_slot, rows_bf.at[core], rows_bf.at[core], "core", 1)

    def rows_landed():
        return copies.copy(rows_slot, rows_bf.at[1 - core], rows_bf.at[1 - core], "core", 1)

    messages.append(Message("rows", ("core", True), width * 1.5 / 4, 1, ["cast"], rows_copy, rows_landed))
    jobs = [
        Job("cast", 0.6, (), cast_rows, 2),
        Job("merge", 0, [("ids1", delta) for delta in range(1, nz)], merge_ids),
        Job("spread", 0, ["merge", *(("ids2", delta) for delta in range(1, ny))], spread_ids),
        *(
            Job(("hits", x, y), 0.4, ["spread", *(("ids3", delta) for delta in range(1, nx))],
                functools.partial(count_hits, x, y), 2)
            for x in range(nx) for y in range(ny)
        ),
    ]
    def queries_of(x, y, count):
        pieces = [held[p // 2, p % 2, x, pl.ds(y, count)].reshape(count * lanes, LANES) for p in range(6)]
        return jnp.concatenate(pieces, axis=1)

    def score_plane(offset):
        x = place.ring("x", offset)
        for y in range(0, ny, 2):
            query = queries_of(x, y, 2)
            tops = []
            for side in range(2):
                block = lax.dot_general(
                    rows_bf[side], query, (((1,), (1,)), ((), ())), preferred_element_type=jnp.float32
                )
                tops.append(jnp.max(block, axis=0, keepdims=True))
                for k in range(2):
                    scores[x, y + k, side] = block[:, k * lanes : (k + 1) * lanes]
            top = jnp.maximum(tops[0], tops[1])
            for k in range(2):
                part = top[:, k * lanes : (k + 1) * lanes]
                amount = jnp.zeros((1, lanes), jnp.float32)
                for side in range(2):
                    power = jnp.exp(scores[x, y + k, side] - part)
                    scores[x, y + k, side] = power
                    amount += jnp.sum(power, axis=0, keepdims=True)
                stat[0, x, 0, y + k : y + k + 1] = part
                stat[0, x, 1, y + k : y + k + 1] = amount

    rings = (("z", stat_z), ("y", stat_y), ("x", stat_x))

    def combine(stage, offset):
        x = slice(None) if offset is None else place.ring("x", offset)
        slots = rings[stage][1]
        count = sizes[rings[stage][0]] - 1
        top = stat[stage, x, 0]
        for slot in range(count):
            top = jnp.maximum(top, slots[slot, x, 0])
        amount = stat[stage, x, 1] * jnp.exp(stat[stage, x, 0] - top)
        for slot in range(count):
            amount += slots[slot, x, 1] * jnp.exp(slots[slot, x, 0] - top)
        if stage < 2:
            stat[stage + 1, x, 0] = top
            stat[stage + 1, x, 1] = amount
        else:
            log_total = top + jnp.log(amount)
            logs[x] = log_total
            factor[x] = jnp.exp(stat[0, x, 0] - log_total)

    def stat_message(stage, offset, delta, deps):
        slot = copies.slot()
        axis, slots = rings[stage]

        def copy():
            x = slice(None) if offset is None else place.ring("x", offset)
            return copies.copy(slot, stat.at[stage, x], slots.at[delta - 1, x], axis, delta)

        return Message(
            ("stat", stage, offset, delta), place.link(axis, delta), 4, min(delta, sizes[axis] - delta), deps, copy
        )

    order = offsets(nx)
    for offset in order:
        deps = [m.key for m in messages if reaches(m.key, offset, sizes["x"])]
        jobs.append(Job(("score", offset), 1.3, deps, functools.partial(score_plane, offset), 1))
    for stage, (axis, _) in enumerate(rings):
        deltas = range(1, sizes[axis])
        for offset in order if stage < 2 else [None]:
            if stage == 0:
                deps = [("score", offset)]
            elif stage == 1:
                deps = [("combine", 0, offset)]
            else:
                deps = [("combine", 1, offset) for offset in order]
            messages += [stat_message(stage, offset, delta, deps) for delta in deltas]
            jobs.append(Job(
                ("combine", stage, offset), 0.2, [("stat", stage, offset, delta) for delta in deltas],
                functools.partial(combine, stage, offset),
            ))

    order = order[::-1]

    def query_plane(offset):
        x = place.ring("x", offset)

        def step(pair, carry):
            y = 2 * pair
            out = None
            for side in range(2):
                for k in range(2):
                    share = 1.0 / jnp.sum((ids_x[x, y + k] >= 0).astype(jnp.float32), axis=0, keepdims=True)
                    scale = factor[x, pl.ds(y + k, 1)]
                    hits = grads[x, y + k, side].astype(jnp.float32)
                    grads[x, y + k, side] = (scores[x, y + k, side] * scale - hits * share).astype(jnp.bfloat16)
                left = jnp.concatenate([grads[x, y, side], grads[x, y + 1, side]], axis=1)
                term = lax.dot_general(
                    left, rows_bf[side], (((0,), (0,)), ((), ())), preferred_element_type=jnp.float32
                )
                out = term if out is None else out + term
            for piece in range(6):
                total[piece // 2, piece % 2, x, pl.ds(y, 2)] = out[
                    :, piece * LANES : (piece + 1) * LANES
                ].reshape(2, nz, 16, LANES)
            return carry

        lax.fori_loop(0, ny // 2, step, 0)

    def row_step(side, out, offset):
        x = place.ring("x", offset)
        left = jnp.concatenate([grads[x, y, side] for y in range(ny)], axis=1)
        term = jnp.dot(left, queries_of(x, 0, ny), preferred_element_type=jnp.float32)
        if offset == order[0]:
            out[...] = term
        else:
            out[...] += term

    def row_sum():
        row_grad_ref[...] += row_land[...]

    parts = [
        reduce_messages(copies, part, total, landings[3 * part : 3 * part + 3]) for part in range(3)
    ]
    messages += [m for group in itertools.zip_longest(*parts) for m in group if m is not None]
    row_slot = copies.slot()
    messages.append(Message(
        "row", ("core", True), width * 3 / 4, 1, [("theirs", order[-1])],
        lambda: copies.copy(row_slot, row_part, row_land, "core", 1),
    ))
    every_hit = [("hits", x, y) for x in range(nx) for y in range(ny)]
    jobs += [
        Job(("query", offset), 1.6, [("combine", 2, None), *every_hit], functools.partial(query_plane, offset), 1)
        for offset in order
    ]
    for name, side, out in (("theirs", 1 - core, row_part), ("ours", core, row_grad_ref)):
        before = []
        for offset in order:
            jobs.append(Job(
                (name, offset), 0.7, [("query", offset), *before], functools.partial(row_step, side, out, offset), 2
            ))
            before = [(name, offset)]
    jobs.append(Job("sum", 0.5, ["row", ("ours", order[-1])], row_sum, 2))
    sent = play(messages, jobs)
    log_ref[...] = jnp.broadcast_to(logs[at["x"], pl.ds(at["y"], 1)], (8, lanes))
    for piece in range(6):
        query_grad_ref[:, piece * LANES : (piece + 1) * LANES] = total[
            piece // 2, piece % 2, at["x"], at["y"], at["z"]
        ]
    for copy in sent:
        copy.wait_send()


def exchange_step(queries, label_rows, slot_ids, counts, sizes):
    nx, ny, nz = (sizes[axis] for axis in "xyz")
    width, depth = label_rows.shape
    lanes = nz * 16
    f32, bf16 = jnp.float32, jnp.bfloat16
    landings = []
    for first, second, third in ORDERS:
        n1, n2, n3 = sizes[first], sizes[second], sizes[third]
        landings += [
            pltpu.VMEM((n2, 2, n1 // 2, 2, n3, 16, LANES), f32),
            pltpu.VMEM((2, n2 // 2, 2, n3, 16, LANES), f32),
            pltpu.VMEM((n3 - 1, 2, 16, LANES), f32),
        ]
    dma = pltpu.SemaphoreType.DMA
    vmem = pl.BlockSpec(memory_space=pltpu.VMEM)
    return pl.pallas_call(
        functools.partial(kernel, sizes),
        out_shape=(
            jax.ShapeDtypeStruct((width, depth), f32),
            jax.ShapeDtypeStruct((16, depth), f32),
            jax.ShapeDtypeStruct((8, lanes), f32),
        ),
        in_specs=[pl.BlockSpec(memory_space=pltpu.HBM)] * 4,
        out_specs=(vmem,) * 3,
        scratch_shapes=[
            pltpu.VMEM((2, width, depth), bf16),
            pltpu.VMEM((3, 2, nx, ny, nz, 16, LANES), bf16),
            pltpu.VMEM((nx, ny, 2, width, lanes), f32),
            pltpu.VMEM((nx, ny, 2, width, lanes), bf16),
            pltpu.VMEM((3, 2, nx, ny, nz, 16, LANES), f32),
            *landings,
            pltpu.VMEM((16, depth), bf16),
            pltpu.VMEM((width, depth), f32),
            pltpu.VMEM((8, 16), jnp.int32),
            pltpu.VMEM((1, 16), jnp.int32),
            pltpu.VMEM((nz - 1, 8, lanes), jnp.int32),
            pltpu.VMEM((nx, ny, 8, lanes), jnp.int32),
            pltpu.VMEM((8, lanes), jnp.int32),
            pltpu.VMEM((ny, 8, lanes), jnp.int32),
            pltpu.VMEM((3, nx, 2, ny, lanes), f32),
            pltpu.VMEM((nx - 1, nx, 2, ny, lanes), f32),
            pltpu.VMEM((ny - 1, nx, 2, ny, lanes), f32),
            pltpu.VMEM((nz - 1, nx, 2, ny, lanes), f32),
            pltpu.VMEM((nx, ny, lanes), f32),
            pltpu.VMEM((nx, ny, lanes), f32),
            pltpu.VMEM((width, depth), f32),
            pltpu.VMEM((width, depth), f32),
            dma((COPIES,)), dma((COPIES,)), dma((4,)),
        ],
        compiler_params=pltpu.CompilerParams(
            collective_id=0, has_side_effects=True, vmem_limit_bytes=60 << 20
        ),
        name="classifier_step",
    )(queries, label_rows, slot_ids, counts)


def adam_kernel(nz, grad_ref, rows_ref, first_ref, second_ref, query_ref, log_ref,
                new_rows_ref, new_first_ref, new_second_ref, query_grad_ref, own_ref,
                grad, rows, first, second, new_rows, new_first, new_second, load, store):
    count = grad.shape[0] // ADAM_TILES
    loads = []
    for number in range(ADAM_TILES):
        tile = pl.ds(number * count, count)
        pairs = ((grad_ref, grad), (rows_ref, rows), (first_ref, first), (second_ref, second))
        loads.append([
            pltpu.make_async_copy(source.at[tile], target.at[tile], load.at[number, k])
            for k, (source, target) in enumerate(pairs)
        ])
    for copy in itertools.chain(*loads[:ADAM_AHEAD]):
        copy.start()
    query_grad_ref[...] = query_ref[...]
    z = lax.rem(lax.axis_index("inner") // 2, nz)
    own = jnp.zeros((1, 16), jnp.float32)
    for k in range(nz):
        own = jnp.where(z == k, log_ref[0:1, k * 16 : (k + 1) * 16], own)
    own_ref[...] = own
    stores = []
    for number in range(ADAM_TILES):
        tile = pl.ds(number * count, count)
        for copy in itertools.chain(*loads[number + ADAM_AHEAD : number + ADAM_AHEAD + 1]):
            copy.start()
        for copy in loads[number]:
            copy.wait()
        gradient = grad[tile]
        moment = 0.9 * first[tile] + 0.1 * gradient
        spread = 0.999 * second[tile] + 0.001 * gradient * gradient
        update = moment / (1.0 - 0.9**10) / (jnp.sqrt(spread / (1.0 - 0.999**10)) + 1e-08)
        new_rows[tile] = rows[tile] - 0.001 * update
        new_first[tile] = moment
        new_second[tile] = spread
        pairs = ((new_rows, new_rows_ref), (new_first, new_first_ref), (new_second, new_second_ref))
        for k, (source, target) in enumerate(pairs):
            copy = pltpu.make_async_copy(source.at[tile], target.at[tile], store.at[number, k])
            copy.start()
            stores.append(copy)
    for copy in stores:
        copy.wait()


def adam_step(row_grad, label_rows, first_moment, second_moment, query_grad, logs, nz):
    f32 = jnp.float32
    whole = jax.ShapeDtypeStruct(label_rows.shape, f32)
    vmem = pl.BlockSpec(memory_space=pltpu.VMEM)
    hbm = pl.BlockSpec(memory_space=pltpu.HBM)
    return pl.pallas_call(
        functools.partial(adam_kernel, nz),
        out_shape=(whole, whole, whole, jax.ShapeDtypeStruct(query_grad.shape, f32), jax.ShapeDtypeStruct((1, 16), f32)),
        in_specs=[hbm] * 4 + [vmem] * 2,
        out_specs=(hbm, hbm, hbm, vmem, vmem),
        scratch_shapes=[
            *[pltpu.VMEM(label_rows.shape, f32)] * 7,
            pltpu.SemaphoreType.DMA((ADAM_TILES, 4)), pltpu.SemaphoreType.DMA((ADAM_TILES, 3)),
        ],
        compiler_params=pltpu.CompilerParams(vmem_limit_bytes=60 << 20),
        name="adam_step",
    )(row_grad, label_rows, first_moment, second_moment, query_grad, logs)


def shards(sizes, queries, label_rows, first_moment, second_moment, positive_ids, positive_counts):
    row_grad, query_grad, logs = exchange_step(
        queries, label_rows, positive_ids.T, positive_counts.reshape(1, -1), sizes
    )
    new_rows, new_first, new_second, query_grad, own_total = adam_step(
        row_grad, label_rows, first_moment, second_moment, query_grad, logs, sizes["z"]
    )
    return (new_rows, new_first, new_second, query_grad, own_total.reshape(-1))


def solution(mesh):
    sizes = {"x": X, "y": mesh.shape["outer"], "z": Z}
    rows = P(("inner", "outer"), None)
    return jax.shard_map(
        functools.partial(shards, sizes),
        mesh=mesh,
        in_specs=(rows, rows, rows, rows, rows, P(("inner", "outer"))),
        out_specs=(rows, rows, rows, rows, P(("inner", "outer"))),
        check_vma=False,
    )
```

```python
import functools
import itertools

import jax
import jax.numpy as jnp
from jax import lax
from jax.experimental import pallas as pl
from jax.experimental.pallas import tpu as pltpu
from jax.sharding import PartitionSpec as P

X, Z = 4, 8
LANES = 128
MESH = pl.DeviceIdType.MESH
ORDERS = ("xyz", "yxz", "zxy")
GATHER_ORDERS = ("zyx", "zxy", "yxz")
LINK_RATE = 46.0
COPIES = 320
ADAM_TILES = 4
ADAM_AHEAD = 4


class Place:
    def __init__(self, sizes):
        self.sizes = sizes
        inner = lax.axis_index("inner")
        self.core = lax.rem(inner, 2)
        self.at = {
            "x": inner // (2 * sizes["z"]),
            "z": lax.rem(inner // 2, sizes["z"]),
            "y": lax.axis_index("outer"),
        }

    def ring(self, axis, delta):
        n = self.sizes[axis]
        return lax.rem(self.at[axis] + delta % n, n)

    def link(self, axis, delta):
        return (axis, 0 < delta % self.sizes[axis] <= self.sizes[axis] // 2)

    def device(self, axis, delta):
        at = dict(self.at)
        core = self.core
        if axis == "core":
            core = 1 - core
        else:
            at[axis] = self.ring(axis, delta)
        return ((at["x"] * self.sizes["z"] + at["z"]) * 2 + core, at["y"])


def slab(ref, half, fixed):
    whole = slice(None)
    first = whole if half is None else half
    return ref.at[(first, *(fixed.get(axis, whole) for axis in "xyz"))]


def offsets(n):
    half = n // 2
    return [0, *(sign * d for d in range(1, half) for sign in (1, -1)), half]


def offset_of(n, offset):
    offset = (offset + n) % n
    return offset if offset <= n // 2 else offset - n


class Message:
    def __init__(self, key, link, kib, hops, deps, copy, landed=None, arrive=None, needs=()):
        self.key, self.link, self.kib, self.hops, self.deps = key, link, kib, hops, set(deps)
        self.needs = set(needs)
        self.copy, self.landed, self.arrive = copy, landed or copy, arrive


class Job:
    def __init__(self, key, cost, deps, work, rank=0):
        self.key, self.cost, self.deps, self.work, self.rank = key, cost, set(deps), work, rank


def play(messages, jobs, sent):
    now, free, arrivals, done, number = 0.0, {}, [], set(), itertools.count()
    waiting, jobs = list(messages), list(jobs)

    def start_ready():
        for message in list(waiting):
            if message.deps <= done:
                waiting.remove(message)
                copy = message.copy()
                copy.start()
                sent.append((message.key if isinstance(message.key, str) else message.key[0], copy))
                begin = max(now, free.get(message.link, 0.0))
                free[message.link] = begin + message.kib * (message.hops if message.hops < 3 else 1.5) / LINK_RATE
                arrivals.append((free[message.link] + 2.7 + 0.6 * message.hops, next(number), message))

    def run(job):
        nonlocal now
        job.work()
        now += job.cost
        done.add(job.key)

    start_ready()
    while arrivals or jobs:
        landing = sorted(entry for entry in arrivals if entry[2].needs <= done)
        gap = landing[0][0] - now if landing else 1e9
        ready = [job for job in jobs if job.deps <= done and gap > (-1e9, 0.0, 0.6 * job.cost)[job.rank]]
        if ready:
            job = min(ready, key=lambda job: job.rank)
            jobs.remove(job)
            run(job)
        else:
            arrivals.remove(landing[0])
            when, _, message = landing[0]
            now = max(now, when) + 0.05
            message.landed().wait_recv()
            if message.arrive is not None:
                message.arrive()
                now += message.kib / 2000
            done.add(message.key)
        start_ready()
    assert not waiting


class Copies:
    def __init__(self, place, send, recv):
        self.place, self.send, self.recv, self.used = place, send, recv, 0

    def slot(self):
        self.used += 1
        return self.used - 1

    def copy(self, slot, source, target, axis, delta):
        return pltpu.make_async_remote_copy(
            src_ref=source, dst_ref=target, send_sem=self.send.at[slot], recv_sem=self.recv.at[slot],
            device_id=self.place.device(axis, delta), device_id_type=MESH,
        )


def reaches(key, offset, n):
    if key == "rows":
        return True
    if key[0] != "in":
        return False
    _, part, phase, *rest = key
    order = GATHER_ORDERS[part]
    if phase < 3:
        return True
    if order[2] == "x":
        _, way, step = rest
        return offset_of(n, step if way else -step) == offset
    return order[1] != "x" or rest[0] == offset


def gather_messages(copies, part, held):
    place = copies.place
    held = held.at[part]
    first, second, third = GATHER_ORDERS[part]
    at, sizes = place.at, place.sizes
    out = []

    def add(key, axis, delta, kib, hops, deps, block_from):
        slot = copies.slot()
        make = lambda back: copies.copy(slot, block_from(back), block_from(back), axis, delta)
        out.append(Message(
            key, place.link(axis, delta), kib, hops, deps,
            functools.partial(make, 0), functools.partial(make, 1),
        ))

    base = 16 * 2 * LANES * 2 / 1024
    for delta in range(1, sizes[first]):
        far = min(delta, sizes[first] - delta)

        def block(back, delta=delta):
            fixed = dict(at)
            fixed[first] = place.ring(first, -delta * back)
            return slab(held, None, fixed)

        add(("in", part, 1, delta), first, delta, base, far, (), block)
    start = [("in", part, 1, delta) for delta in range(1, sizes[first])]
    base *= sizes[first]
    for delta in range(1, sizes[second]):

        def block(back, delta=delta):
            return slab(held, None, {third: at[third], second: place.ring(second, -delta * back)})

        add(("in", part, 2, delta), second, delta, base, min(delta, sizes[second] - delta), start, block)
    far = sizes[third] // 2
    for offset in offsets(sizes[second]):
        for step in range(1, far + 1):
            for way, sign in enumerate((1, -1)):

                def block(back, offset=offset, step=step, way=way, sign=sign):
                    fixed = {
                        second: place.ring(second, offset),
                        third: place.ring(third, -sign * (step - 1 + back)),
                    }
                    return slab(held, way if step == far else None, fixed)

                if step > 1:
                    deps = [("in", part, 3, offset, way, step - 1)]
                elif offset == 0:
                    deps = start
                else:
                    deps = [("in", part, 2, -offset % sizes[second])]
                add(("in", part, 3, offset, way, step), third, sign, base / (1 + (step == far)), 1, deps, block)
    return out


def reduce_messages(copies, part, total, landings):
    place = copies.place
    total = total.at[part]
    first, second, third = ORDERS[part]
    at, sizes = place.at, place.sizes
    out = []

    def add(key, axis, delta, kib, hops, deps, source, landed, mine, needs=()):
        slot = copies.slot()

        def arrive():
            mine()[...] += landed[...]

        out.append(Message(
            key, place.link(axis, delta), kib, hops, deps,
            lambda: copies.copy(slot, source(), landed, axis, delta), None, arrive, needs,
        ))

    base = sizes[third] * 16 * 2 * LANES * 4 / 1024
    reach, far = sizes[first] // 2, sizes[second] // 2
    for number, offset in enumerate(offsets(sizes[second])[::-1]):
        for step in range(1, reach + 1):
            for way, sign in enumerate((1, -1)):

                def block(ahead, offset=offset, step=step, way=way, sign=sign):
                    fixed = {
                        second: place.ring(second, offset),
                        first: place.ring(first, sign * (reach - step + ahead)),
                    }
                    return slab(total, way if step == 1 else None, fixed)

                landed = landings[0].at[number, way, step - 1]
                if step == 1:
                    landed = landed.at[0]
                deps = [("out", part, 1, offset, way, step - 1)] if step > 1 else []
                if first == "x":
                    ahead, here = ([offset_of(sizes["x"], sign * (reach - step + k))] for k in (1, 0))
                else:
                    ahead = here = [offset] if second == "x" else offsets(sizes["x"])
                deps += [("query", plane) for plane in ahead]
                add(("out", part, 1, offset, way, step), first, sign, base / (1 + (step == 1)), 1, deps,
                    functools.partial(block, 1), landed, functools.partial(block, 0),
                    [("query", plane) for plane in here])
    for step in range(1, far + 1):
        for way, sign in enumerate((1, -1)):

            def block(ahead, step=step, way=way, sign=sign):
                fixed = {first: at[first], second: place.ring(second, sign * (far - step + ahead))}
                return slab(total, way if step == 1 else None, fixed)

            landed = landings[1].at[way, step - 1]
            if step == 1:
                landed = landed.at[0]
            offset = offset_of(sizes[second], sign * (far - step + 1))
            deps = [("out", part, 1, offset, w, reach) for w in range(2)]
            if step > 1:
                deps.append(("out", part, 2, way, step - 1))
            add(("out", part, 2, way, step), second, sign, base / (1 + (step == 1)), 1, deps,
                functools.partial(block, 1), landed, functools.partial(block, 0))
    base /= sizes[third]
    deps = [("out", part, 1, 0, w, reach) for w in range(2)] + [("out", part, 2, w, far) for w in range(2)]
    for delta in range(1, sizes[third]):

        def block(ahead, delta=delta):
            fixed = dict(at)
            fixed[third] = place.ring(third, delta * ahead)
            return slab(total, None, fixed)

        add(("out", part, 3, delta), third, delta, base, min(delta, sizes[third] - delta), deps,
            functools.partial(block, 1), landings[2].at[delta - 1], functools.partial(block, 0))
    return out


def kernel(
    sizes, q_ref, rows_ref, ids_ref, count_ref, row_grad_ref, query_grad_ref, log_ref,
    rows_bf, held, scores, grads, total, *rest,
):
    landings, rest = rest[:9], rest[9:]
    (own, rows, ids_in, count_in, ids_z, ids_x, ids_own, ids_ys, stat, stat_x, stat_y, stat_z, logs, factor, row_part, row_land,
     send, recv, load) = rest
    place = Place(sizes)
    nx, ny, nz = sizes["x"], sizes["y"], sizes["z"]
    width = rows_ref.shape[0]
    lanes = nz * 16
    loading = [
        pltpu.make_async_copy(source, target, load.at[k])
        for k, (source, target) in enumerate(
            ((rows_ref, rows), (q_ref, own), (ids_ref, ids_in), (count_ref, count_in))
        )
    ]
    for copy in loading:
        copy.start()
    at = place.at
    core = place.core

    barrier = pltpu.get_barrier_semaphore()
    peers = [("core", 1)] + [(axis, delta) for axis in "xyz" for delta in range(1, sizes[axis])]
    for axis, delta in peers:
        pl.semaphore_signal(barrier, inc=1, device_id=place.device(axis, delta), device_id_type=MESH)

    for copy in loading[1:]:
        copy.wait()
    for piece in range(6):
        held[piece // 2, piece % 2, at["x"], at["y"], at["z"]] = own[:, piece * LANES : (piece + 1) * LANES]
    lane = lax.broadcasted_iota(jnp.int32, (8, lanes), 1)
    valid = lax.broadcasted_iota(jnp.int32, (8, 16), 0) < count_in[...]
    own_ids = jnp.where(valid, ids_in[...], -1)
    ids_own[...] = jnp.where(lane // 16 == at["z"], jnp.concatenate([own_ids] * nz, axis=1), -1)

    def cast_rows():
        loading[0].wait()
        rows_bf[core] = rows[...].astype(jnp.bfloat16)

    pl.semaphore_wait(barrier, len(peers))

    copies = Copies(place, send, recv)

    def merge_ids():
        merged = ids_own[...]
        for slot in range(nz - 1):
            merged = jnp.maximum(merged, ids_z[slot])
        ids_ys[at["y"]] = merged

    def spread_ids():
        ids_x[at["x"]] = ids_ys[...]

    def count_hits(x, y):
        ids = ids_x[x, y]
        start = ((at["x"] * nz + at["z"]) * 2 * ny + at["y"]) * width

        def step(side, carry):
            label = start + side * (ny * width) + lax.broadcasted_iota(jnp.int32, (width, lanes), 0)
            hits = jnp.zeros((width, lanes), jnp.float32)
            for slot in range(8):
                hits += jnp.where(ids[slot : slot + 1] == label, 1.0, 0.0)
            grads[x, y, side] = hits.astype(jnp.bfloat16)
            return carry

        lax.fori_loop(0, 2, step, 0)

    def id_message(kind, axis, delta, kib, source, target, deps):
        slot = copies.slot()
        return Message(
            (kind, delta), place.link(axis, delta), kib, min(delta, sizes[axis] - delta), deps,
            lambda: copies.copy(slot, source, target(0), axis, delta),
            lambda: copies.copy(slot, source, target(1), axis, delta),
        )

    messages = [
        id_message("ids1", "z", delta, 4, ids_own, lambda back, delta=delta: ids_z.at[delta - 1], ())
        for delta in range(1, nz)
    ]
    messages += [
        id_message("ids2", "y", delta, 4, ids_ys.at[at["y"]],
                   lambda back, delta=delta: ids_ys.at[place.ring("y", -delta * back)], ["merge"])
        for delta in range(1, ny)
    ]
    messages += [
        id_message("ids3", "x", delta, 16, ids_x.at[at["x"]],
                   lambda back, delta=delta: ids_x.at[place.ring("x", -delta * back)], ["spread"])
        for delta in range(1, nx)
    ]
    parts = [gather_messages(copies, part, held) for part in range(3)]
    messages += [m for group in itertools.zip_longest(*parts) for m in group if m is not None]
    rows_slot = copies.slot()

    def rows_copy():
        return copies.copy(rows_slot, rows_bf.at[core], rows_bf.at[core], "core", 1)

    def rows_landed():
        return copies.copy(rows_slot, rows_bf.at[1 - core], rows_bf.at[1 - core], "core", 1)

    messages.append(Message("rows", ("core", True), width * 1.5 / 4, 1, ["cast"], rows_copy, rows_landed))
    jobs = [
        Job("cast", 0.6, (), cast_rows, 2),
        Job("merge", 0, [("ids1", delta) for delta in range(1, nz)], merge_ids),
        Job("spread", 0, ["merge", *(("ids2", delta) for delta in range(1, ny))], spread_ids),
        *(
            Job(("hits", x, y), 0.4, ["spread", *(("ids3", delta) for delta in range(1, nx))],
                functools.partial(count_hits, x, y), 2)
            for x in range(nx) for y in range(ny)
        ),
    ]
    def queries_of(x, y, count):
        pieces = [held[p // 2, p % 2, x, pl.ds(y, count)].reshape(count * lanes, LANES) for p in range(6)]
        return jnp.concatenate(pieces, axis=1)

    def score_plane(offset):
        x = place.ring("x", offset)
        for y in range(0, ny, 2):
            query = queries_of(x, y, 2)
            tops = []
            for side in range(2):
                block = lax.dot_general(
                    rows_bf[side], query, (((1,), (1,)), ((), ())), preferred_element_type=jnp.float32
                )
                tops.append(jnp.max(block, axis=0, keepdims=True))
                for k in range(2):
                    scores[x, y + k, side] = block[:, k * lanes : (k + 1) * lanes]
            top = jnp.maximum(tops[0], tops[1])
            for k in range(2):
                part = top[:, k * lanes : (k + 1) * lanes]
                amount = jnp.zeros((1, lanes), jnp.float32)
                for side in range(2):
                    power = jnp.exp(scores[x, y + k, side] - part)
                    scores[x, y + k, side] = power
                    amount += jnp.sum(power, axis=0, keepdims=True)
                stat[0, x, 0, y + k : y + k + 1] = part
                stat[0, x, 1, y + k : y + k + 1] = amount

    rings = (("z", stat_z), ("y", stat_y), ("x", stat_x))

    def combine(stage, offset):
        x = slice(None) if offset is None else place.ring("x", offset)
        slots = rings[stage][1]
        count = sizes[rings[stage][0]] - 1
        top = stat[stage, x, 0]
        for slot in range(count):
            top = jnp.maximum(top, slots[slot, x, 0])
        amount = stat[stage, x, 1] * jnp.exp(stat[stage, x, 0] - top)
        for slot in range(count):
            amount += slots[slot, x, 1] * jnp.exp(slots[slot, x, 0] - top)
        if stage < 2:
            stat[stage + 1, x, 0] = top
            stat[stage + 1, x, 1] = amount
        else:
            log_total = top + jnp.log(amount)
            logs[x] = log_total
            factor[x] = jnp.exp(stat[0, x, 0] - log_total)

    def stat_message(stage, offset, delta, deps):
        slot = copies.slot()
        axis, slots = rings[stage]

        def copy():
            x = slice(None) if offset is None else place.ring("x", offset)
            return copies.copy(slot, stat.at[stage, x], slots.at[delta - 1, x], axis, delta)

        return Message(
            ("stat", stage, offset, delta), place.link(axis, delta), 4, min(delta, sizes[axis] - delta), deps, copy
        )

    order = offsets(nx)
    for offset in order:
        deps = [m.key for m in messages if reaches(m.key, offset, sizes["x"])]
        jobs.append(Job(("score", offset), 1.3, deps, functools.partial(score_plane, offset), 1))
    for stage, (axis, _) in enumerate(rings):
        deltas = range(1, sizes[axis])
        for offset in order if stage < 2 else [None]:
            if stage == 0:
                deps = [("score", offset)]
            elif stage == 1:
                deps = [("combine", 0, offset)]
            else:
                deps = [("combine", 1, offset) for offset in order]
            messages += [stat_message(stage, offset, delta, deps) for delta in deltas]
            jobs.append(Job(
                ("combine", stage, offset), 0.2, [("stat", stage, offset, delta) for delta in deltas],
                functools.partial(combine, stage, offset),
            ))

    order = order[::-1]

    def query_plane(offset):
        x = place.ring("x", offset)

        def step(pair, carry):
            y = 2 * pair
            out = None
            for side in range(2):
                for k in range(2):
                    share = 1.0 / jnp.sum((ids_x[x, y + k] >= 0).astype(jnp.float32), axis=0, keepdims=True)
                    scale = factor[x, pl.ds(y + k, 1)]
                    hits = grads[x, y + k, side].astype(jnp.float32)
                    grads[x, y + k, side] = (scores[x, y + k, side] * scale - hits * share).astype(jnp.bfloat16)
                left = jnp.concatenate([grads[x, y, side], grads[x, y + 1, side]], axis=1)
                term = lax.dot_general(
                    left, rows_bf[side], (((0,), (0,)), ((), ())), preferred_element_type=jnp.float32
                )
                out = term if out is None else out + term
            for piece in range(6):
                total[piece // 2, piece % 2, x, pl.ds(y, 2)] = out[
                    :, piece * LANES : (piece + 1) * LANES
                ].reshape(2, nz, 16, LANES)
            return carry

        lax.fori_loop(0, ny // 2, step, 0)

    def row_step(side, out, offset):
        x = place.ring("x", offset)
        left = jnp.concatenate([grads[x, y, side] for y in range(ny)], axis=1)
        term = jnp.dot(left, queries_of(x, 0, ny), preferred_element_type=jnp.float32)
        if offset == order[0]:
            out[...] = term
        else:
            out[...] += term

    def row_sum():
        row_grad_ref[...] += row_land[...]

    parts = [
        reduce_messages(copies, part, total, landings[3 * part : 3 * part + 3]) for part in range(3)
    ]
    messages += [m for group in itertools.zip_longest(*parts) for m in group if m is not None]
    row_slot = copies.slot()
    messages.append(Message(
        "row", ("core", True), width * 3 / 4, 1, [("theirs", order[-1])],
        lambda: copies.copy(row_slot, row_part, row_land, "core", 1),
    ))
    every_hit = [("hits", x, y) for x in range(nx) for y in range(ny)]
    jobs += [
        Job(("query", offset), 1.6, [("combine", 2, None), *every_hit], functools.partial(query_plane, offset), 1)
        for offset in order
    ]
    for name, side, out in (("theirs", 1 - core, row_part), ("ours", core, row_grad_ref)):
        before = []
        for offset in order:
            jobs.append(Job(
                (name, offset), 0.7, [("query", offset), *before], functools.partial(row_step, side, out, offset), 2
            ))
            before = [(name, offset)]
    jobs.append(Job("sum", 0.5, ["row", ("ours", order[-1])], row_sum, 2))
    sent = []

    def drain():
        early = [entry for entry in sent if entry[0] not in ("out", "row")]
        sent[:] = [entry for entry in sent if entry[0] in ("out", "row")]
        for _, copy in early:
            copy.wait_send()

    jobs.append(Job("drain", 1.0, [("theirs", order[-1])], drain, 2))
    play(messages, jobs, sent)
    log_ref[...] = jnp.broadcast_to(logs[at["x"], pl.ds(at["y"], 1)], (8, lanes))
    for piece in range(6):
        query_grad_ref[:, piece * LANES : (piece + 1) * LANES] = total[
            piece // 2, piece % 2, at["x"], at["y"], at["z"]
        ]
    for _, copy in sent:
        copy.wait_send()


def exchange_step(queries, label_rows, slot_ids, counts, sizes):
    nx, ny, nz = (sizes[axis] for axis in "xyz")
    width, depth = label_rows.shape
    lanes = nz * 16
    f32, bf16 = jnp.float32, jnp.bfloat16
    landings = []
    for first, second, third in ORDERS:
        n1, n2, n3 = sizes[first], sizes[second], sizes[third]
        landings += [
            pltpu.VMEM((n2, 2, n1 // 2, 2, n3, 16, LANES), f32),
            pltpu.VMEM((2, n2 // 2, 2, n3, 16, LANES), f32),
            pltpu.VMEM((n3 - 1, 2, 16, LANES), f32),
        ]
    dma = pltpu.SemaphoreType.DMA
    vmem = pl.BlockSpec(memory_space=pltpu.VMEM)
    return pl.pallas_call(
        functools.partial(kernel, sizes),
        out_shape=(
            jax.ShapeDtypeStruct((width, depth), f32),
            jax.ShapeDtypeStruct((16, depth), f32),
            jax.ShapeDtypeStruct((8, lanes), f32),
        ),
        in_specs=[pl.BlockSpec(memory_space=pltpu.HBM)] * 4,
        out_specs=(vmem,) * 3,
        scratch_shapes=[
            pltpu.VMEM((2, width, depth), bf16),
            pltpu.VMEM((3, 2, nx, ny, nz, 16, LANES), bf16),
            pltpu.VMEM((nx, ny, 2, width, lanes), f32),
            pltpu.VMEM((nx, ny, 2, width, lanes), bf16),
            pltpu.VMEM((3, 2, nx, ny, nz, 16, LANES), f32),
            *landings,
            pltpu.VMEM((16, depth), bf16),
            pltpu.VMEM((width, depth), f32),
            pltpu.VMEM((8, 16), jnp.int32),
            pltpu.VMEM((1, 16), jnp.int32),
            pltpu.VMEM((nz - 1, 8, lanes), jnp.int32),
            pltpu.VMEM((nx, ny, 8, lanes), jnp.int32),
            pltpu.VMEM((8, lanes), jnp.int32),
            pltpu.VMEM((ny, 8, lanes), jnp.int32),
            pltpu.VMEM((3, nx, 2, ny, lanes), f32),
            pltpu.VMEM((nx - 1, nx, 2, ny, lanes), f32),
            pltpu.VMEM((ny - 1, nx, 2, ny, lanes), f32),
            pltpu.VMEM((nz - 1, nx, 2, ny, lanes), f32),
            pltpu.VMEM((nx, ny, lanes), f32),
            pltpu.VMEM((nx, ny, lanes), f32),
            pltpu.VMEM((width, depth), f32),
            pltpu.VMEM((width, depth), f32),
            dma((COPIES,)), dma((COPIES,)), dma((4,)),
        ],
        compiler_params=pltpu.CompilerParams(
            collective_id=0, has_side_effects=True, vmem_limit_bytes=60 << 20
        ),
        name="classifier_step",
    )(queries, label_rows, slot_ids, counts)


def adam_kernel(nz, grad_ref, rows_ref, first_ref, second_ref, query_ref, log_ref,
                new_rows_ref, new_first_ref, new_second_ref, query_grad_ref, own_ref,
                grad, rows, first, second, new_rows, new_first, new_second, load, store):
    count = grad.shape[0] // ADAM_TILES
    loads = []
    for number in range(ADAM_TILES):
        tile = pl.ds(number * count, count)
        pairs = ((grad_ref, grad), (rows_ref, rows), (first_ref, first), (second_ref, second))
        loads.append([
            pltpu.make_async_copy(source.at[tile], target.at[tile], load.at[number, k])
            for k, (source, target) in enumerate(pairs)
        ])
    for copy in itertools.chain(*loads[:ADAM_AHEAD]):
        copy.start()
    query_grad_ref[...] = query_ref[...]
    z = lax.rem(lax.axis_index("inner") // 2, nz)
    own = jnp.zeros((1, 16), jnp.float32)
    for k in range(nz):
        own = jnp.where(z == k, log_ref[0:1, k * 16 : (k + 1) * 16], own)
    own_ref[...] = own
    stores = []
    for number in range(ADAM_TILES):
        tile = pl.ds(number * count, count)
        for copy in itertools.chain(*loads[number + ADAM_AHEAD : number + ADAM_AHEAD + 1]):
            copy.start()
        for copy in loads[number]:
            copy.wait()
        gradient = grad[tile]
        moment = 0.9 * first[tile] + 0.1 * gradient
        spread = 0.999 * second[tile] + 0.001 * gradient * gradient
        update = moment / (1.0 - 0.9**10) / (jnp.sqrt(spread / (1.0 - 0.999**10)) + 1e-08)
        new_rows[tile] = rows[tile] - 0.001 * update
        new_first[tile] = moment
        new_second[tile] = spread
        pairs = ((new_rows, new_rows_ref), (new_first, new_first_ref), (new_second, new_second_ref))
        for k, (source, target) in enumerate(pairs):
            copy = pltpu.make_async_copy(source.at[tile], target.at[tile], store.at[number, k])
            copy.start()
            stores.append(copy)
    for copy in stores:
        copy.wait()


def adam_step(row_grad, label_rows, first_moment, second_moment, query_grad, logs, nz):
    f32 = jnp.float32
    whole = jax.ShapeDtypeStruct(label_rows.shape, f32)
    vmem = pl.BlockSpec(memory_space=pltpu.VMEM)
    hbm = pl.BlockSpec(memory_space=pltpu.HBM)
    return pl.pallas_call(
        functools.partial(adam_kernel, nz),
        out_shape=(whole, whole, whole, jax.ShapeDtypeStruct(query_grad.shape, f32), jax.ShapeDtypeStruct((1, 16), f32)),
        in_specs=[hbm] * 4 + [vmem] * 2,
        out_specs=(hbm, hbm, hbm, vmem, vmem),
        scratch_shapes=[
            *[pltpu.VMEM(label_rows.shape, f32)] * 7,
            pltpu.SemaphoreType.DMA((ADAM_TILES, 4)), pltpu.SemaphoreType.DMA((ADAM_TILES, 3)),
        ],
        compiler_params=pltpu.CompilerParams(vmem_limit_bytes=60 << 20),
        name="adam_step",
    )(row_grad, label_rows, first_moment, second_moment, query_grad, logs)


def shards(sizes, queries, label_rows, first_moment, second_moment, positive_ids, positive_counts):
    row_grad, query_grad, logs = exchange_step(
        queries, label_rows, positive_ids.T, positive_counts.reshape(1, -1), sizes
    )
    new_rows, new_first, new_second, query_grad, own_total = adam_step(
        row_grad, label_rows, first_moment, second_moment, query_grad, logs, sizes["z"]
    )
    return (new_rows, new_first, new_second, query_grad, own_total.reshape(-1))


def solution(mesh):
    sizes = {"x": X, "y": mesh.shape["outer"], "z": Z}
    rows = P(("inner", "outer"), None)
    return jax.shard_map(
        functools.partial(shards, sizes),
        mesh=mesh,
        in_specs=(rows, rows, rows, rows, rows, P(("inner", "outer"))),
        out_specs=(rows, rows, rows, rows, P(("inner", "outer"))),
        check_vma=False,
    )
```
